512 devices in a mesh: pt: 128 (over z, x, core), cen: 4 (over y).
Axes of the slice: x: 4, y: 4, z: 16, core: 2. Of those that a mesh axis runs over, the one named last changes fastest.
Arguments:
- points: bfloat16 [196608, 1024], P('pt'), may hold values from -8 to 8
- lengths: int32 [768], P('pt'), may hold values from 1 to 256, 147456 in all
- candidates: int32 [768, 16], P('pt'), may hold values from 0 to 255, as said below
- centroids: bfloat16 [256, 256, 1024], P('pt', 'cen'), may hold values from -6 to 6
Outputs:
- updated: bfloat16 [256, 256, 1024], P('pt', 'cen')
- masses: float32 [256, 256], P('pt', 'cen')
- log_partition: float32 [196608], P('pt')
The draws below stay inside these ranges and needn't reach their ends.
Inputs may be any that keep to these rules, and one draw needn't show every extreme that they name: `candidates`: the 16 ids of a point block are different, and each names a centroid block held by a device of pt at most 4 positions away on either side, counted circularly, from the device of pt that holds the point block; block b is held by index b // 2 of pt.
All inputs are finite; a program needn't handle non-finite values. No bound on the sum of `lengths` on one device may be relied on, other than what follows from the above.
Results may differ from the reference program's by a relative error of at most 0.005.
Values may be sent and summed in bfloat16 or wider, within the bound.
No kernel may reach another device: no remote copies, remote signals or barrier semaphores. Data moves between devices by JAX's collectives and lax.ppermute only.
A program may use at most 64 MiB of HBM per device.

```python
import math
import jax
import jax.numpy as jnp
import numpy as np
from jax import lax

D = 1024
BLOCK = 256
CANDS = 16
REACH = 4
CB_DEV = 2
PB_DEV = 6
NPB = 768
POINTS = 196608
NCB = 256


def centre_values(key):
    key = jax.random.fold_in(key, 101)
    return jax.random.truncated_normal(key, -6.0, 6.0, (NCB, BLOCK, D), jnp.float32) * D ** (-0.5)


def pick_candidates(key):
    key = jax.random.fold_in(key, 202)
    devices = NCB // CB_DEV
    span_count = min(2 * REACH + 1, devices)
    home_dev = jnp.arange(NPB, dtype=jnp.int32) // PB_DEV
    slot_ids = jnp.arange(span_count * CB_DEV, dtype=jnp.int32)
    owner_dev = (home_dev[:, None] - REACH + slot_ids[None, :] // CB_DEV) % devices
    block_ids = owner_dev * CB_DEV + slot_ids[None, :] % CB_DEV
    scores = jax.random.randint(key, (NPB, span_count * CB_DEV), 0, 1 << 20, dtype=jnp.int32) * 64 + slot_ids[None, :]
    chosen = lax.top_k(scores, CANDS)[1]
    return jnp.take_along_axis(block_ids, chosen, 1).astype(jnp.int32)


def draw_centroids(key, part):
    return centre_values(key).astype(jnp.bfloat16)


def draw_candidates(key, part):
    return pick_candidates(key)


def draw_points(key, part):
    key = jax.random.fold_in(key, 303)
    values_base = jax.random.truncated_normal(key, -6.0, 6.0, (NPB, BLOCK, D), jnp.float32) * D ** (-0.5)
    return values_base.reshape(NPB * BLOCK, D).astype(jnp.bfloat16)


def length_profile(count, total, bound, lean):
    weights = [(1 << 20) // math.isqrt(standing ** lean) + 1 for standing in range(2, count + 1)]
    surplus, counts = total - bound - (count - 1), [1] * (count - 1)
    while surplus > 0:
        movable = [i for i in range(count - 1) if counts[i] < bound]
        whole, left = sum([weights[i] for i in movable]), surplus
        for i in movable:
            addition = min(bound - counts[i], max(1, left * weights[i] // whole), surplus)
            counts[i] = counts[i] + addition
            surplus = surplus - addition
    return np.array([bound] + counts)


def uneven_parts(stream_key, number_of, total, bound, lean):
    if number_of == 2:
        one = jax.random.randint(stream_key, (), max(1, total - bound), min(bound, total - 1) + 1)
        return jnp.stack([one, total - one])
    sizes = jnp.asarray(length_profile(number_of, total, bound, lean), jnp.int32)
    couples = (number_of - 1) // 2
    giver, taker = sizes[1:1 + 2 * couples:2], sizes[2:2 + 2 * couples:2]
    room = jnp.minimum(giver - 1, bound - taker)
    shifted = jax.random.randint(jax.random.fold_in(stream_key, 1), (couples,), 0, 1 << 20) % (room + 1)
    sizes = sizes.at[1:1 + 2 * couples:2].set(giver - shifted).at[2:2 + 2 * couples:2].set(taker + shifted)
    return sizes[jax.random.permutation(jax.random.fold_in(stream_key, 2), number_of)]


def setup_inputs(seed: int = 0) -> dict:
    seeds = jax.random.split(jax.random.key(seed), 5)
    return {
        "points": draw_points(jax.random.fold_in(seeds[4], 71), 0),
        "lengths": uneven_parts(seeds[1], NPB, NPB * (3 * BLOCK // 4), BLOCK, 2).astype(jnp.int32),
        "candidates": draw_candidates(jax.random.fold_in(seeds[4], 71), 0),
        "centroids": draw_centroids(jax.random.fold_in(seeds[4], 71), 0),
    }


sharpness_factor = 1.5
prior_mass = 1.0

def reference(points, lengths, candidates, centroids):
    sharpness = sharpness_factor * math.sqrt(D)
    squares = lax.optimization_barrier(jnp.sum(jnp.square(centroids.astype(jnp.float32)), -1))
    point_blocks = points.reshape(NPB, BLOCK, D)

    def visit(running, inputs):
        moments, masses = running
        sample_rows, chosen, live_len = inputs
        gathered = centroids[chosen].reshape(CANDS * BLOCK, D)
        products = jnp.dot(sample_rows, gathered.T, preferred_element_type=jnp.float32)
        logits = (2.0 * products - squares[chosen].reshape(1, CANDS * BLOCK)) * sharpness
        row_max = lax.optimization_barrier(jnp.max(logits, -1, keepdims=True))
        power_term = jnp.exp(logits - row_max)
        row_sum = lax.optimization_barrier(jnp.sum(power_term, -1, keepdims=True))
        live_mask = (jnp.arange(BLOCK, dtype=jnp.int32) < live_len).astype(jnp.float32)[:, None]
        weights = (power_term / row_sum * live_mask).astype(jnp.bfloat16)
        weighted_features = jnp.dot(weights.T, sample_rows, preferred_element_type=jnp.float32).reshape(CANDS, BLOCK, D)
        moments = moments.at[chosen].add(weighted_features)
        masses = masses.at[chosen].add(lax.optimization_barrier(jnp.sum(weights.astype(jnp.float32), 0)).reshape(CANDS, BLOCK))
        return ((moments, masses), (row_max + jnp.log(row_sum))[:, 0])
    initial = (jnp.zeros((NCB, BLOCK, D), jnp.float32), jnp.zeros((NCB, BLOCK), jnp.float32))
    (moments, masses), log_rows = lax.scan(visit, initial, (point_blocks, candidates, lengths))
    updated = ((moments + prior_mass * centroids.astype(jnp.float32)) / (masses + prior_mass)[..., None]).astype(jnp.bfloat16)
    return (updated, masses, log_rows.reshape(POINTS))
```

```python
import math

import jax
import jax.numpy as jnp
from jax import lax
from jax.experimental import pallas as pl
from jax.experimental.pallas import tpu as pltpu
from jax.sharding import Mesh
from jax.sharding import PartitionSpec as P

D = 1024
CORES = 2
BLOCK = 256
LANES = 128
CHUNK = 512
FAR = -1e30

sharpness_factor = 1.5
prior_mass = 1.0
SHARP = sharpness_factor * math.sqrt(D)


def log_weights(mask_ref, points, rows_ref, square_ref, first_block, centre_rows):
    products = lax.dot_general(
        rows_ref[...], points, (((1,), (1,)), ((), ())), preferred_element_type=jnp.float32
    )
    count = rows_ref.shape[0] // centre_rows
    columns = []
    for part in range(points.shape[0] // BLOCK):
        pieces = []
        for b in range(count):
            rows = slice(b * centre_rows, (b + 1) * centre_rows)
            bias = square_ref[rows, :] + mask_ref[first_block + part, b]
            bias = jnp.concatenate([bias] * (BLOCK // LANES), 1)
            pieces.append(
                products[rows, part * BLOCK : (part + 1) * BLOCK] * (2.0 * SHARP) + bias
            )
        columns.append(jnp.concatenate(pieces, 0))
    return jnp.concatenate(columns, 1)


def fill_rows(shards, rows_ref, square_ref):
    size = shards[0].shape[0]
    for n, shard in enumerate(shards):
        value = shard[...]
        rows_ref[n * size : (n + 1) * size, :] = value
        wide = value.astype(jnp.float32)
        squares = jnp.sum(wide * wide, 1, keepdims=True) * (-SHARP)
        square_ref[n * size : (n + 1) * size, :] = jnp.broadcast_to(squares, (size, LANES))


def score_kernel(centre_rows, half, shard_count, has_earlier, *refs):
    mask_ref, core_ref = refs[:2]
    shards = refs[2 : 2 + shard_count]
    own_ref, other_ref = refs[2 + shard_count : 4 + shard_count]
    rest = refs[4 + shard_count :]
    if has_earlier:
        early_max, early_sum, power_ref, max_ref, lse_ref, rows_ref, square_ref = rest
    else:
        power_ref, max_ref, sum_ref, rows_ref, square_ref = rest
    step = pl.program_id(0)

    @pl.when(step == 0)
    def _():
        fill_rows(shards, rows_ref, square_ref)

    def chunk(points):
        logits = log_weights(
            mask_ref, points, rows_ref, square_ref, step * (CHUNK // BLOCK), centre_rows
        )
        top = jnp.max(logits, 0, keepdims=True)
        power = jnp.exp(logits - top)
        total = jnp.sum(power, 0, keepdims=True)
        power_ref[...] = power.astype(jnp.bfloat16)
        for n in range(CHUNK // LANES):
            group = step * (CHUNK // LANES) + n
            lanes = slice(n * LANES, (n + 1) * LANES)
            max_here, sum_here = top[:, lanes], total[:, lanes]
            max_ref[pl.ds(group, 1), :] = max_here
            if has_earlier:
                max_before = early_max[pl.ds(group, 1), :]
                sum_before = early_sum[pl.ds(group, 1), :]
                both = jnp.maximum(max_here, max_before)
                summed = sum_here * jnp.exp(max_here - both) + sum_before * jnp.exp(
                    max_before - both
                )
                groups = half // LANES
                place = jnp.where(
                    core_ref[0] == 0, group, lax.rem(group + groups, 2 * groups)
                )
                lse_ref[pl.ds(place, 1), :] = both + jnp.log(summed)
            else:
                sum_ref[pl.ds(group, 1), :] = sum_here

    steps = half // CHUNK

    @pl.when(step < steps)
    def _():
        chunk(own_ref[...])

    @pl.when(step >= steps)
    def _():
        chunk(other_ref[...])


def whole(shape):
    return pl.BlockSpec(shape, lambda i: (0,) * len(shape))


def score(shards, mask, core, own, other, centre_rows, earlier=None):
    size = shards[0].shape[0]
    half = own.shape[0]
    steps = half // CHUNK
    rows = size * len(shards)
    groups = 2 * half // LANES
    stat = jax.ShapeDtypeStruct((groups, LANES), jnp.float32)
    smem = pl.BlockSpec(memory_space=pltpu.SMEM)
    in_specs = [smem, smem]
    in_specs += [whole((size, D))] * len(shards)
    in_specs += [
        pl.BlockSpec((CHUNK, D), lambda i: (jnp.minimum(i, steps - 1), 0)),
        pl.BlockSpec((CHUNK, D), lambda i: (jnp.maximum(i - steps, 0), 0)),
    ]
    args = [mask, core, *shards, own, other]
    if earlier is not None:
        in_specs += [whole((groups, LANES))] * 2
        args += list(earlier)

    def kernel(*refs):
        score_kernel(centre_rows, half, len(shards), earlier is not None, *refs)

    return pl.pallas_call(
        kernel,
        grid=(2 * steps,),
        in_specs=in_specs,
        out_specs=[pl.BlockSpec((rows, CHUNK), lambda i: (0, i))]
        + [whole((groups, LANES))] * 2,
        out_shape=[jax.ShapeDtypeStruct((rows, 2 * half), jnp.bfloat16), stat, stat],
        scratch_shapes=[
            pltpu.VMEM((rows, D), jnp.bfloat16),
            pltpu.VMEM((rows, LANES), jnp.float32),
        ],
        compiler_params=pltpu.CompilerParams(vmem_limit_bytes=40 << 20),
        cost_estimate=pl.CostEstimate(
            flops=2 * rows * 2 * half * D,
            bytes_accessed=2 * half * D * 2 + rows * half * 4,
            transcendentals=rows * 2 * half,
        ),
    )(*args)


def moments_kernel(first, dests, size, half, keep, *refs):
    core_ref, all_ref, max_ref, live_ref, power_ref, own_ref, other_ref = refs[:7]
    outs = refs[7 : 7 + dests + (2 if keep else 0) + (1 if first else 0)]
    scale_ref, total_ref, mass_ref = refs[-3:]
    step = pl.program_id(0)
    steps = half // CHUNK
    groups = half // LANES

    @pl.when(step == 0)
    def _():
        parts = all_ref[...]
        top = jnp.max(parts, 0)
        lse = top + jnp.log(jnp.sum(jnp.exp(parts - top[None]), 0))
        here = jnp.where(core_ref[0] == 0, lse[:groups], lse[groups:])
        there = jnp.where(core_ref[0] == 0, lse[groups:], lse[:groups])
        ordered = jnp.concatenate([here, there], 0)
        scale_ref[...] = jnp.exp(max_ref[...] - ordered) * live_ref[...]
        if first:
            outs[-1][...] = here
        total_ref[...] = jnp.zeros_like(total_ref)
        mass_ref[...] = jnp.zeros_like(mass_ref)

    def chunk(points):
        pieces = []
        mass = mass_ref[...]
        for n in range(CHUNK // LANES):
            scale = scale_ref[pl.ds(step * (CHUNK // LANES) + n, 1), :]
            power = power_ref[:, n * LANES : (n + 1) * LANES].astype(jnp.float32)
            weights = (power * scale).astype(jnp.bfloat16)
            mass += weights.astype(jnp.float32)
            pieces.append(weights)
        mass_ref[...] = mass
        total_ref[...] += jnp.dot(
            jnp.concatenate(pieces, 1), points, preferred_element_type=jnp.float32
        )

    @pl.when(step < steps)
    def _():
        chunk(own_ref[...])

    @pl.when(step >= steps)
    def _():
        chunk(other_ref[...])

    @pl.when(step == 2 * steps - 1)
    def _():
        for n in range(dests + (1 if keep else 0)):
            rows = slice(n * size, (n + 1) * size)
            mass = jnp.sum(jnp.transpose(mass_ref[rows, :]), 0, keepdims=True)
            mass = jnp.broadcast_to(mass, (8, size))
            if n < dests:
                out = outs[n]
                for j in range(D // LANES):
                    out[j * size : (j + 1) * size, :] = total_ref[
                        rows, j * LANES : (j + 1) * LANES
                    ].astype(jnp.bfloat16)
                coarse = mass.astype(jnp.bfloat16).astype(jnp.float32)
                out[D // LANES * size :, :] = jnp.concatenate(
                    [coarse, mass - coarse], 0
                ).astype(jnp.bfloat16)
            else:
                outs[dests][...] = total_ref[rows, :]
                outs[dests + 1][...] = mass


def message_rows(size):
    return D // LANES * size + 16


def moments(core, everyone, top, live, power, own, other, size, dests, keep, first):
    half = own.shape[0]
    steps = half // CHUNK
    rows = power.shape[0]
    groups = 2 * half // LANES
    smem = pl.BlockSpec(memory_space=pltpu.SMEM)
    message = (message_rows(size), LANES)
    out_shape = [jax.ShapeDtypeStruct(message, jnp.bfloat16)] * dests
    if keep:
        out_shape += [
            jax.ShapeDtypeStruct((size, D), jnp.float32),
            jax.ShapeDtypeStruct((8, size), jnp.float32),
        ]
    if first:
        out_shape += [jax.ShapeDtypeStruct((half // LANES, LANES), jnp.float32)]

    def kernel(*refs):
        moments_kernel(first, dests, size, half, keep, *refs)

    return pl.pallas_call(
        kernel,
        grid=(2 * steps,),
        in_specs=[
            smem,
            whole(everyone.shape),
            whole((groups, LANES)),
            whole((groups, LANES)),
            pl.BlockSpec((rows, CHUNK), lambda i: (0, i)),
            pl.BlockSpec((CHUNK, D), lambda i: (jnp.minimum(i, steps - 1), 0)),
            pl.BlockSpec((CHUNK, D), lambda i: (jnp.maximum(i - steps, 0), 0)),
        ],
        out_specs=[whole(s.shape) for s in out_shape],
        out_shape=out_shape,
        scratch_shapes=[
            pltpu.VMEM((groups, LANES), jnp.float32),
            pltpu.VMEM((rows, D), jnp.float32),
            pltpu.VMEM((rows, LANES), jnp.float32),
        ],
        compiler_params=pltpu.CompilerParams(vmem_limit_bytes=40 << 20),
        cost_estimate=pl.CostEstimate(
            flops=2 * rows * 2 * half * D,
            bytes_accessed=2 * half * D * 2 + rows * half * 4,
            transcendentals=0,
        ),
    )(core, everyone, top, live, power, own, other)


def finish_kernel(size, *refs):
    home_ref, home_mass_ref, centre_ref = refs[:3]
    arrived = refs[3:-2]
    updated_ref, mass_out_ref = refs[-2:]
    tail = D // LANES * size
    mass = home_mass_ref[...]
    for message in arrived:
        sent = message[tail:, :].astype(jnp.float32)
        mass += sent[:8] + sent[8:]
    mass_out_ref[...] = mass
    inverse = 1.0 / (mass[:1] + prior_mass)
    inverse = jnp.transpose(jnp.broadcast_to(inverse, (LANES, size)))
    for j in range(D // LANES):
        lanes = slice(j * LANES, (j + 1) * LANES)
        total = home_ref[:, lanes] + prior_mass * centre_ref[:, lanes].astype(jnp.float32)
        for message in arrived:
            total += message[j * size : (j + 1) * size, :].astype(jnp.float32)
        updated_ref[:, lanes] = (total * inverse).astype(jnp.bfloat16)


def finish(home, home_mass, centre, arrived):
    size = centre.shape[0]
    return pl.pallas_call(
        lambda *refs: finish_kernel(size, *refs),
        out_shape=[
            jax.ShapeDtypeStruct((size, D), jnp.bfloat16),
            jax.ShapeDtypeStruct((8, size), jnp.float32),
        ],
        compiler_params=pltpu.CompilerParams(vmem_limit_bytes=40 << 20),
    )(home, home_mass, centre, *arrived)


def local(points, lengths, candidates, centroids):
    chips = lax.axis_size("chip")
    cen_count = lax.axis_size("cen")
    chip = lax.axis_index("chip")
    core = lax.axis_index("core")
    local_blocks, centre_rows, _ = centroids.shape
    size = local_blocks * centre_rows
    half = points.shape[0]

    def moved(value, steps):
        return lax.ppermute(value, "chip", [(c, (c + steps) % chips) for c in range(chips)])

    centre = centroids.reshape(size, D)
    near = [moved(centre, 1), moved(centre, -1)]
    far = [moved(centre, 2), moved(centre, -2)]
    swap = [(0, 1), (1, 0)]
    other = lax.ppermute(points, "core", swap)
    facts = jnp.concatenate([candidates, lengths[:, None]], 1)
    facts = jnp.concatenate([facts, lax.ppermute(facts, "core", swap)], 0)
    candidates, lengths = facts[:, :-1], facts[:, -1]

    owners = (chip + jnp.array([-1, 1, 0, -2, 2], jnp.int32)) % chips
    blocks = (
        (owners * CORES + core)[:, None] * local_blocks
        + jnp.arange(local_blocks, dtype=jnp.int32)[None, :]
    ).reshape(-1)
    chosen = jnp.any(candidates[:, None, :] == blocks[None, :, None], -1)
    mask = jnp.where(chosen, 0.0, FAR).astype(jnp.float32)
    places = jnp.arange(2 * half, dtype=jnp.int32).reshape(-1, BLOCK) % BLOCK
    live = (places < lengths[:, None]).astype(jnp.float32).reshape(-1, LANES)
    core_here = core.astype(jnp.int32).reshape(1)

    split = 3 * local_blocks
    near_power, near_max, near_sum = score(
        [*near, centre], mask[:, :split], core_here, points, other, centre_rows
    )
    far_power, far_max, lse_here = score(
        far, mask[:, split:], core_here, points, other, centre_rows, (near_max, near_sum)
    )
    count = CORES * cen_count
    everyone = lax.all_to_all(
        jnp.broadcast_to(lse_here, (count, *lse_here.shape)), ("core", "cen"), 0, 0
    )
    far_before, far_after, lse = moments(
        core_here, everyone, far_max, live, far_power, points, other, size, 2, False, True
    )
    arrived = [moved(far_before, -2), moved(far_after, 2)]
    near_before, near_after, home, home_mass = moments(
        core_here, everyone, near_max, live, near_power, points, other, size, 2, True, False
    )
    arrived += [moved(near_before, -1), moved(near_after, 1)]
    updated, masses = finish(home, home_mass, centre, arrived)
    return (
        updated.reshape(centroids.shape),
        masses[0].reshape(local_blocks, centre_rows),
        lse.reshape(-1),
    )


def solution(mesh):
    pt, cen = mesh.axis_names
    split = Mesh(
        mesh.devices.reshape(mesh.shape[pt] // CORES, CORES, mesh.shape[cen]),
        ("chip", "core", "cen"),
    )
    whole_pt = ("chip", "core")
    return jax.shard_map(
        local,
        mesh=split,
        in_specs=(P(whole_pt, None), P(whole_pt), P(whole_pt, None), P(whole_pt, "cen", None)),
        out_specs=(P(whole_pt, "cen", None), P(whole_pt, "cen"), P(whole_pt)),
        check_vma=False,
    )
```

```python
import math

import jax
import jax.numpy as jnp
from jax import lax
from jax.experimental import pallas as pl
from jax.experimental.pallas import tpu as pltpu
from jax.sharding import Mesh
from jax.sharding import PartitionSpec as P

D = 1024
CORES = 2
ROW = 4
BLOCK = 256
LANES = 128
CHUNK = 512
GROUPS = CHUNK // LANES
FAR = -1e30
VMEM_LIMIT = 24 << 20

sharpness_factor = 1.5
prior_mass = 1.0
SHARP = sharpness_factor * math.sqrt(D) / math.log(2.0)

SMEM = pl.BlockSpec(memory_space=pltpu.SMEM)
VMEM = pl.BlockSpec(memory_space=pltpu.VMEM)


def compiler_params():
    return pltpu.CompilerParams(vmem_limit_bytes=VMEM_LIMIT)


def fill_rows(shards, rows_ref, square_ref, first):
    size = shards[0].shape[0]
    for n, shard in enumerate(shards, first):
        for r in range(0, size, 32):
            value = shard[r : r + 32, :]
            at = slice(n * size + r, n * size + r + 32)
            rows_ref[at, :] = value
            wide = value.astype(jnp.float32)
            squares = jnp.sum(wide * wide, 1, keepdims=True) * (-SHARP)
            square_ref[at, :] = jnp.broadcast_to(squares, (32, LANES))


def reached(name, chip, chips):
    low = lax.rem(chip, ROW) < ROW // 2
    step = {
        "before": chips - 1,
        "after": 1,
        "own": 0,
        "row": jnp.where(low, 2, chips - 2),
        "beyond": jnp.where(low, chips - 2, 2),
    }[name]
    return lax.rem(chip + step, chips)


def fill_mask(names, chips, local_blocks, chip_ref, core_ref, candidate_ref, mask_ref):
    count = candidate_ref.shape[1]
    own, other = candidate_ref[core_ref[0]], candidate_ref[1 - core_ref[0]]
    held = 0
    for name in names:
        owner = reached(name, chip_ref[0], chips) * CORES + core_ref[0]
        for n in range(local_blocks):
            block = owner * local_blocks + n
            for at, ids in ((0, own), (count, other)):
                here = jnp.where(ids == block, 0.0, FAR).astype(jnp.float32)
                here = jnp.max(here, 1, keepdims=True)
                mask_ref[held, at : at + count, :] = jnp.broadcast_to(here, (count, LANES))
            held += 1


def folded(op, tile):
    parts = [tile[r : r + 8] for r in range(0, tile.shape[0], 8)]
    while len(parts) > 1:
        parts = [op(a, b) for a, b in zip(parts[::2], parts[1::2])]
    return parts[0]


def score_kernel(names, chips, local_blocks, later, *refs):
    chip_ref, core_ref, candidate_ref = refs[:3]
    own_ref, other_ref = refs[3:5]
    shards = list(refs[5 : 5 + len(names)])
    rest = refs[5 + len(names) :]
    copies = []
    if later:
        early_max, early_sum, length_ref, power_ref, max_ref, message_ref = rest[:6]
        sum_ref = rest[6]
    else:
        power_ref, max_ref, sum_ref, kept_ref, centre_ref, semaphores = rest[:6]
        copies = [
            pltpu.make_async_copy(shards[-1], centre_ref, semaphores.at[0]),
            pltpu.make_async_copy(own_ref, kept_ref, semaphores.at[1]),
        ]
        own_ref, shards[-1] = kept_ref, centre_ref
    rows_ref, square_ref, mask_ref, product_ref = rest[-4:]
    half = own_ref.shape[0]
    steps = half // CHUNK
    centre_rows = shards[0].shape[0] // local_blocks
    blocks = len(names) * local_blocks

    for copy in copies:
        copy.start()
    if copies:
        fill_rows(shards[:-1], rows_ref, square_ref, 0)
        copies[0].wait()
        fill_rows(shards[-1:], rows_ref, square_ref, len(shards) - 1)
    else:
        fill_rows(shards, rows_ref, square_ref, 0)

    def multiply(step):
        source, first = (other_ref, step) if step < steps else (own_ref, step - steps)
        if step == steps and copies:
            copies[1].wait()
        product_ref[step % 2] = lax.dot_general(
            rows_ref[...],
            source[first * CHUNK : (first + 1) * CHUNK, :],
            (((1,), (1,)), ((), ())),
            preferred_element_type=jnp.float32,
        )

    multiply(0)
    fill_mask(names, chips, local_blocks, chip_ref, core_ref, candidate_ref, mask_ref)
    for step in range(2 * steps):
        if step + 1 < 2 * steps:
            multiply(step + 1)
        held = product_ref.at[step % 2]
        for n in range(GROUPS):
            lanes = slice(n * LANES, (n + 1) * LANES)
            place = (step * CHUNK + half) % (2 * half) + n * LANES
            q = place // BLOCK
            tops = []
            for b in range(blocks):
                rows = slice(b * centre_rows, (b + 1) * centre_rows)
                bias = square_ref[rows, :] + mask_ref[b, q : q + 1, :]
                logits = held[rows, lanes] * (2.0 * SHARP) + bias
                held[rows, lanes] = logits
                tops.append(folded(jnp.maximum, logits))
            top = tops[0]
            for more in tops[1:]:
                top = jnp.maximum(top, more)
            top = jnp.max(top, 0, keepdims=True)
            total = jnp.zeros((8, LANES), jnp.float32)
            for b in range(blocks):
                rows = slice(b * centre_rows, (b + 1) * centre_rows)
                power = jnp.exp2(held[rows, lanes] - top)
                total += folded(jnp.add, power)
                power_ref[rows, place : place + LANES] = power.astype(jnp.bfloat16)
            group = place // LANES
            max_ref[group : group + 1, :] = top
            sum_ref[group : group + 1, :] = jnp.sum(total, 0, keepdims=True)

    if later:
        both = jnp.maximum(max_ref[...], early_max[...])
        summed = sum_ref[...] * jnp.exp2(max_ref[...] - both)
        summed += early_sum[...] * jnp.exp2(early_max[...] - both)
        lse = both + jnp.log2(summed)
        groups = half // LANES
        here, there = lse[:groups], lse[groups:]
        first = core_ref[0] == 0
        lengths = [
            jnp.full((1, LANES), length_ref[q].astype(jnp.float32)) for q in range(half // BLOCK)
        ]
        lengths += [jnp.zeros((1, LANES), jnp.float32)] * (-len(lengths) % 8)
        message = jnp.concatenate(
            [jnp.where(first, here, there), jnp.where(first, there, here), *lengths], 0
        )
        for n in range(message_ref.shape[0]):
            message_ref[n] = message


def score(names, chips, chip, core, candidates, points, shards, local_blocks, later=None):
    size = shards[0].shape[0]
    half = points[0].shape[0]
    rows = size * len(shards)
    groups = 2 * half // LANES
    stat = jax.ShapeDtypeStruct((groups, LANES), jnp.float32)
    out_shape = [jax.ShapeDtypeStruct((rows, 2 * half), jnp.bfloat16), stat]
    scratch = []
    in_specs = [SMEM, SMEM] + [VMEM] * (3 + len(shards))
    args = [chip, core, candidates, *points, *shards]
    if later is None:
        in_specs[3] = in_specs[-1] = pl.BlockSpec(memory_space=pltpu.HBM)
        out_shape += [stat, jax.ShapeDtypeStruct(points[0].shape, points[0].dtype)]
        scratch += [pltpu.VMEM((size, D), shards[0].dtype), pltpu.SemaphoreType.DMA((2,))]
    else:
        early, lengths, copies = later
        in_specs += [VMEM, VMEM, SMEM]
        args += [*early, lengths]
        spare = -(-(half // BLOCK) // 8) * 8
        out_shape += [jax.ShapeDtypeStruct((copies, groups + spare, LANES), jnp.float32)]
        scratch += [pltpu.VMEM((groups, LANES), jnp.float32)]
    point_blocks = -(-(2 * half // BLOCK) // 8) * 8

    def kernel(*refs):
        score_kernel(names, chips, local_blocks, later is not None, *refs)

    return pl.pallas_call(
        kernel,
        in_specs=in_specs,
        out_specs=[VMEM] * len(out_shape),
        out_shape=out_shape,
        scratch_shapes=scratch
        + [
            pltpu.VMEM((rows, D), jnp.bfloat16),
            pltpu.VMEM((rows, LANES), jnp.float32),
            pltpu.VMEM((len(shards) * local_blocks, point_blocks, LANES), jnp.float32),
            pltpu.VMEM((2, rows, CHUNK), jnp.float32),
        ],
        compiler_params=compiler_params(),
        cost_estimate=pl.CostEstimate(
            flops=2 * rows * 2 * half * D,
            bytes_accessed=2 * half * D * 2 + rows * half * 4,
            transcendentals=rows * 2 * half,
        ),
    )(*args)


def write_message(out, total_ref, mass):
    size = total_ref.shape[0]
    for j in range(D // LANES):
        out[j * size : (j + 1) * size, :] = total_ref[:, j * LANES : (j + 1) * LANES].astype(
            jnp.bfloat16
        )
    coarse = mass.astype(jnp.bfloat16).astype(jnp.float32)
    out[D // LANES * size :, :] = jnp.concatenate([coarse, mass - coarse], 0).astype(jnp.bfloat16)


def merge_kernel(total_ref, mass_ref, arrived_ref, out_ref):
    size = total_ref.shape[0]
    tail = D // LANES * size
    for j in range(D // LANES):
        rows = slice(j * size, (j + 1) * size)
        total = total_ref[:, j * LANES : (j + 1) * LANES] + arrived_ref[rows, :].astype(jnp.float32)
        out_ref[rows, :] = total.astype(jnp.bfloat16)
    sent = arrived_ref[tail:, :].astype(jnp.float32)
    mass = mass_ref[...] + sent[:8] + sent[8:]
    coarse = mass.astype(jnp.bfloat16).astype(jnp.float32)
    out_ref[tail:, :] = jnp.concatenate([coarse, mass - coarse], 0).astype(jnp.bfloat16)


def merged(total, mass, arrived):
    return pl.pallas_call(
        merge_kernel,
        in_specs=[VMEM] * 3,
        out_specs=VMEM,
        out_shape=jax.ShapeDtypeStruct(arrived.shape, arrived.dtype),
        compiler_params=compiler_params(),
    )(total, mass, arrived)


def moments_kernel(sources, sent, size, keep, first, *refs):
    core_ref, all_ref, own_ref, other_ref = refs[:4]
    tops, powers = refs[4:6], refs[6:8]
    outs = refs[8:-4]
    scale_ref, total_ref, mass_ref, weight_ref = refs[-4:]
    half = own_ref.shape[0]
    steps = half // CHUNK
    groups = half // LANES
    at_zero = core_ref[0] == 0

    parts = all_ref[:, : 2 * groups, :]
    top = jnp.max(parts, 0)
    lse = top + jnp.log2(jnp.sum(jnp.exp2(parts - top[None]), 0))
    here = jnp.where(at_zero, lse[:groups], lse[groups:])
    there = jnp.where(at_zero, lse[groups:], lse[:groups])
    for n, top_ref in enumerate(tops):
        scale_ref[n] = jnp.exp2(top_ref[...] - jnp.concatenate([here, there], 0))
    if first:
        outs[-1][...] = here * math.log(2.0)
    copies = all_ref.shape[0] // CORES
    lane = lax.broadcasted_iota(jnp.int32, (1, LANES), 1).astype(jnp.float32)

    def weigh(step):
        for at in range(GROUPS):
            group = step * GROUPS + at
            q = group * LANES // BLOCK
            part = (group * LANES % BLOCK) // LANES
            row = 2 * groups + q % (half // BLOCK)
            zero, one = all_ref[0, row : row + 1, :], all_ref[copies, row : row + 1, :]
            mine = q < half // BLOCK
            length = jnp.where(at_zero, zero if mine else one, one if mine else zero)
            live = jnp.where(lane + part * LANES < length, 1.0, 0.0)
            lanes = slice(group * LANES, (group + 1) * LANES)
            for n, (which, start) in enumerate(sources):
                scale = scale_ref[which, group : group + 1, :] * live
                for r in range(0, size, 64):
                    power = powers[which][start + r : start + r + 64, lanes].astype(jnp.float32)
                    weights = (power * scale).astype(jnp.bfloat16)
                    rows = slice(n * size + r, n * size + r + 64)
                    weight_ref[rows, lanes] = weights
                    if group == 0:
                        mass_ref[rows, :] = weights.astype(jnp.float32)
                    else:
                        mass_ref[rows, :] += weights.astype(jnp.float32)

    weigh(0)
    for step in range(2 * steps):
        if step + 1 < 2 * steps:
            weigh(step + 1)
        source, at = (own_ref, step) if step < steps else (other_ref, step - steps)
        part = jnp.dot(
            weight_ref[:, step * CHUNK : (step + 1) * CHUNK],
            source[at * CHUNK : (at + 1) * CHUNK, :],
            preferred_element_type=jnp.float32,
        )
        if step == 0:
            total_ref[...] = part
        else:
            total_ref[...] += part

    for out, n in zip(outs, (*sent, keep)):
        rows = slice(n * size, (n + 1) * size)
        mass = jnp.sum(jnp.transpose(mass_ref[rows, :]), 0, keepdims=True)
        mass = jnp.broadcast_to(mass, (8, size))
        if n == keep:
            out[...] = total_ref[rows, :]
            outs[len(sent) + 1][...] = mass
        else:
            write_message(out, total_ref.at[rows, :], mass)


def moments(core, everyone, points, tops, powers, sources, size, sent, keep, first):
    half = points[0].shape[0]
    rows = len(sources) * size
    groups = 2 * half // LANES
    message = (D // LANES * size + 16, LANES)
    out_shape = [jax.ShapeDtypeStruct(message, jnp.bfloat16)] * len(sent)
    out_shape += [
        jax.ShapeDtypeStruct((size, D), jnp.float32),
        jax.ShapeDtypeStruct((8, size), jnp.float32),
    ]
    if first:
        out_shape += [jax.ShapeDtypeStruct((half // LANES, LANES), jnp.float32)]

    def kernel(*refs):
        moments_kernel(sources, sent, size, keep, first, *refs)

    return pl.pallas_call(
        kernel,
        in_specs=[SMEM] + [VMEM] * 7,
        out_specs=[VMEM] * len(out_shape),
        out_shape=out_shape,
        scratch_shapes=[
            pltpu.VMEM((len(tops), groups, LANES), jnp.float32),
            pltpu.VMEM((rows, D), jnp.float32),
            pltpu.VMEM((rows, LANES), jnp.float32),
            pltpu.VMEM((rows, 2 * half), jnp.bfloat16),
        ],
        compiler_params=compiler_params(),
        cost_estimate=pl.CostEstimate(
            flops=2 * rows * 2 * half * D,
            bytes_accessed=2 * half * D * 2 + rows * half * 4,
            transcendentals=0,
        ),
    )(core, everyone, *points, *tops, *powers)


def finish_kernel(*refs):
    home_ref, home_mass_ref, centre_ref = refs[:3]
    arrived = refs[3:-2]
    updated_ref, mass_out_ref = refs[-2:]
    size = centre_ref.shape[0]
    tail = D // LANES * size
    mass = home_mass_ref[...]
    for message in arrived:
        sent = message[tail:, :].astype(jnp.float32)
        mass += sent[:8] + sent[8:]
    rows, width = mass_out_ref.shape
    for n in range(rows):
        mass_out_ref[n : n + 1, :] = mass[:1, n * width : (n + 1) * width]
    inverse = 1.0 / (mass[:1] + prior_mass)
    inverse = jnp.transpose(jnp.broadcast_to(inverse, (LANES, size)))
    for j in range(D // LANES):
        lanes = slice(j * LANES, (j + 1) * LANES)
        total = home_ref[:, lanes] + prior_mass * centre_ref[:, lanes].astype(jnp.float32)
        for message in arrived:
            total += message[j * size : (j + 1) * size, :].astype(jnp.float32)
        updated_ref[:, lanes] = (total * inverse).astype(jnp.bfloat16)


def finish(home, home_mass, centre, arrived, local_blocks):
    size = centre.shape[0]
    return pl.pallas_call(
        finish_kernel,
        in_specs=[VMEM] * (3 + len(arrived)),
        out_specs=[VMEM] * 2,
        out_shape=[
            jax.ShapeDtypeStruct((size, D), jnp.bfloat16),
            jax.ShapeDtypeStruct((local_blocks, size // local_blocks), jnp.float32),
        ],
        compiler_params=compiler_params(),
    )(home, home_mass, centre, *arrived)


def local(points, lengths, candidates, centroids):
    chips = lax.axis_size("chip")
    copies = CORES * lax.axis_size("cen")
    chip = lax.axis_index("chip").astype(jnp.int32).reshape(1)
    core = lax.axis_index("core").astype(jnp.int32).reshape(1)
    local_blocks, centre_rows, _ = centroids.shape
    size = local_blocks * centre_rows

    def moved(value, step):
        return lax.ppermute(value, "chip", [(c, step(c) % chips) for c in range(chips)])

    def ahead(c):
        return c + 1

    def back(c):
        return c - 1

    def across(c):
        return c // ROW * ROW + (c + ROW // 2) % ROW

    def outward(c):
        return c + ROW if c % ROW < ROW // 2 else c - ROW

    def inward(c):
        return c - ROW if c % ROW < ROW // 2 else c + ROW

    def swapped(value):
        return lax.ppermute(value, "core", [(0, 1), (1, 0)])

    centre = centroids.reshape(size, D)
    row = moved(centre, across)
    near = [moved(centre, ahead), moved(centre, back)]
    beyond = moved(row, outward)
    other = swapped(points)
    candidates = lax.all_gather(candidates, "core")

    first_power, first_max, first_sum, kept = score(
        ("row", "own"),
        chips,
        chip,
        core,
        candidates,
        [pltpu.with_memory_space_constraint(points, pltpu.HBM), other],
        [row, pltpu.with_memory_space_constraint(centre, pltpu.HBM)],
        local_blocks,
    )
    points = [kept, other]
    last_power, last_max, message = score(
        ("before", "after", "beyond"),
        chips,
        chip,
        core,
        candidates,
        points,
        [*near, beyond],
        local_blocks,
        ((first_max, first_sum), lengths, copies),
    )
    everyone = lax.all_to_all(message, ("core", "cen"), 0, 0)
    tops, powers = (first_max, last_max), (first_power, last_power)
    beyond, row, row_mass, lse = moments(
        core, everyone, points, tops, powers, ((1, 2 * size), (0, 0)), size, (0,), 1, True
    )
    beyond = moved(beyond, inward)
    before, after, home, home_mass = moments(
        core, everyone, points, tops, powers, ((1, 0), (1, size), (0, size)), size, (0, 1), 2, False
    )
    arrived = [moved(before, back), moved(after, ahead)]
    arrived += [moved(merged(row, row_mass, beyond), across)]
    updated, masses = finish(home, home_mass, centre, arrived, local_blocks)
    return updated.reshape(centroids.shape), masses, lse.reshape(-1)


def solution(mesh):
    pt, cen = mesh.axis_names
    split = Mesh(
        mesh.devices.reshape(mesh.shape[pt] // CORES, CORES, mesh.shape[cen]),
        ("chip", "core", "cen"),
    )
    whole_pt = ("chip", "core")
    return jax.shard_map(
        local,
        mesh=split,
        in_specs=(P(whole_pt, None), P(whole_pt), P(whole_pt, None), P(whole_pt, "cen", None)),
        out_specs=(P(whole_pt, "cen", None), P(whole_pt, "cen"), P(whole_pt)),
        check_vma=False,
    )
```

```python
import math

import jax
import jax.numpy as jnp
from jax import lax
from jax.experimental import pallas as pl
from jax.experimental.pallas import tpu as pltpu
from jax.sharding import Mesh
from jax.sharding import PartitionSpec as P

D = 1024
CORES = 2
ROW = 4
BLOCK = 256
LANES = 128
CHUNK = 512
GROUPS = CHUNK // LANES
FAR = -1e30
VMEM_LIMIT = 24 << 20

sharpness_factor = 1.5
prior_mass = 1.0
SHARP = sharpness_factor * math.sqrt(D) / math.log(2.0)

SMEM = pl.BlockSpec(memory_space=pltpu.SMEM)
VMEM = pl.BlockSpec(memory_space=pltpu.VMEM)


def compiler_params():
    return pltpu.CompilerParams(vmem_limit_bytes=VMEM_LIMIT)


def fill_rows(shards, rows_ref, square_ref, first):
    size = shards[0].shape[0]
    for n, shard in enumerate(shards, first):
        for r in range(0, size, 32):
            value = shard[r : r + 32, :]
            at = slice(n * size + r, n * size + r + 32)
            rows_ref[at, :] = value
            wide = value.astype(jnp.float32)
            squares = jnp.sum(wide * wide, 1, keepdims=True) * (-SHARP)
            square_ref[at, :] = jnp.broadcast_to(squares, (32, LANES))


def reached(name, chip, chips):
    low = lax.rem(chip, ROW) < ROW // 2
    step = {
        "before": chips - 1,
        "after": 1,
        "own": 0,
        "row": jnp.where(low, 2, chips - 2),
        "beyond": jnp.where(low, chips - 2, 2),
    }[name]
    return lax.rem(chip + step, chips)


def fill_mask(names, chips, local_blocks, chip_ref, core_ref, candidate_ref, mask_ref):
    count = candidate_ref.shape[1]
    own, other = candidate_ref[core_ref[0]], candidate_ref[1 - core_ref[0]]
    held = 0
    for name in names:
        owner = reached(name, chip_ref[0], chips) * CORES + core_ref[0]
        for n in range(local_blocks):
            block = owner * local_blocks + n
            for at, ids in ((0, own), (count, other)):
                here = jnp.where(ids == block, 0.0, FAR).astype(jnp.float32)
                here = jnp.max(here, 1, keepdims=True)
                mask_ref[held, at : at + count, :] = jnp.broadcast_to(here, (count, LANES))
            held += 1


def folded(op, tile):
    parts = [tile[r : r + 8] for r in range(0, tile.shape[0], 8)]
    while len(parts) > 1:
        parts = [op(a, b) for a, b in zip(parts[::2], parts[1::2])]
    return parts[0]


def score_kernel(names, chips, local_blocks, later, *refs):
    chip_ref, core_ref, candidate_ref = refs[:3]
    own_ref, other_ref = refs[3:5]
    shards = list(refs[5 : 5 + len(names)])
    rest = refs[5 + len(names) :]
    copies = []
    if later:
        early_max, early_sum, length_ref, power_ref, max_ref, message_ref = rest[:6]
        sum_ref = rest[6]
    else:
        power_ref, max_ref, sum_ref, kept_ref, centre_ref, semaphores = rest[:6]
        copies = [
            pltpu.make_async_copy(shards[-1], centre_ref, semaphores.at[0]),
            pltpu.make_async_copy(own_ref, kept_ref, semaphores.at[1]),
        ]
        own_ref, shards[-1] = kept_ref, centre_ref
    rows_ref, square_ref, mask_ref, product_ref = rest[-4:]
    half = own_ref.shape[0]
    steps = half // CHUNK
    centre_rows = shards[0].shape[0] // local_blocks
    blocks = len(names) * local_blocks

    for copy in copies:
        copy.start()
    if copies:
        fill_rows(shards[:-1], rows_ref, square_ref, 0)
        copies[0].wait()
        fill_rows(shards[-1:], rows_ref, square_ref, len(shards) - 1)
    else:
        fill_rows(shards, rows_ref, square_ref, 0)

    def multiply(step):
        source, first = (other_ref, step) if step < steps else (own_ref, step - steps)
        if step == steps and copies:
            copies[1].wait()
        product_ref[step % 2] = lax.dot_general(
            rows_ref[...],
            source[first * CHUNK : (first + 1) * CHUNK, :],
            (((1,), (1,)), ((), ())),
            preferred_element_type=jnp.float32,
        )

    multiply(0)
    fill_mask(names, chips, local_blocks, chip_ref, core_ref, candidate_ref, mask_ref)
    for step in range(2 * steps):
        if step + 1 < 2 * steps:
            multiply(step + 1)
        held = product_ref.at[step % 2]
        for n in range(GROUPS):
            lanes = slice(n * LANES, (n + 1) * LANES)
            place = (step * CHUNK + half) % (2 * half) + n * LANES
            q = place // BLOCK
            tops = []
            for b in range(blocks):
                rows = slice(b * centre_rows, (b + 1) * centre_rows)
                bias = square_ref[rows, :] + mask_ref[b, q : q + 1, :]
                logits = held[rows, lanes] * (2.0 * SHARP) + bias
                held[rows, lanes] = logits
                tops.append(folded(jnp.maximum, logits))
            top = tops[0]
            for more in tops[1:]:
                top = jnp.maximum(top, more)
            top = jnp.max(top, 0, keepdims=True)
            total = jnp.zeros((8, LANES), jnp.float32)
            for b in range(blocks):
                rows = slice(b * centre_rows, (b + 1) * centre_rows)
                power = jnp.exp2(held[rows, lanes] - top)
                total += folded(jnp.add, power)
                power_ref[rows, place : place + LANES] = power.astype(jnp.bfloat16)
            group = place // LANES
            max_ref[group : group + 1, :] = top
            sum_ref[group : group + 1, :] = jnp.sum(total, 0, keepdims=True)

    if later:
        both = jnp.maximum(max_ref[...], early_max[...])
        summed = sum_ref[...] * jnp.exp2(max_ref[...] - both)
        summed += early_sum[...] * jnp.exp2(early_max[...] - both)
        lse = both + jnp.log2(summed)
        groups = half // LANES
        here, there = lse[:groups], lse[groups:]
        first = core_ref[0] == 0
        lengths = [
            jnp.full((1, LANES), length_ref[q].astype(jnp.float32)) for q in range(half // BLOCK)
        ]
        lengths += [jnp.zeros((1, LANES), jnp.float32)] * (-len(lengths) % 8)
        message = jnp.concatenate(
            [jnp.where(first, here, there), jnp.where(first, there, here), *lengths], 0
        )
        for n in range(message_ref.shape[0]):
            message_ref[n] = message


def score(names, chips, chip, core, candidates, points, shards, local_blocks, later=None):
    size = shards[0].shape[0]
    half = points[0].shape[0]
    rows = size * len(shards)
    groups = 2 * half // LANES
    stat = jax.ShapeDtypeStruct((groups, LANES), jnp.float32)
    out_shape = [jax.ShapeDtypeStruct((rows, 2 * half), jnp.bfloat16), stat]
    scratch = []
    in_specs = [SMEM, SMEM] + [VMEM] * (3 + len(shards))
    args = [chip, core, candidates, *points, *shards]
    if later is None:
        in_specs[3] = in_specs[-1] = pl.BlockSpec(memory_space=pltpu.HBM)
        out_shape += [stat, jax.ShapeDtypeStruct(points[0].shape, points[0].dtype)]
        scratch += [pltpu.VMEM((size, D), shards[0].dtype), pltpu.SemaphoreType.DMA((2,))]
    else:
        early, lengths, copies = later
        in_specs += [VMEM, VMEM, SMEM]
        args += [*early, lengths]
        spare = -(-(half // BLOCK) // 8) * 8
        out_shape += [jax.ShapeDtypeStruct((copies, groups + spare, LANES), jnp.float32)]
        scratch += [pltpu.VMEM((groups, LANES), jnp.float32)]
    point_blocks = -(-(2 * half // BLOCK) // 8) * 8

    def kernel(*refs):
        score_kernel(names, chips, local_blocks, later is not None, *refs)

    return pl.pallas_call(
        kernel,
        in_specs=in_specs,
        out_specs=[VMEM] * len(out_shape),
        out_shape=out_shape,
        scratch_shapes=scratch
        + [
            pltpu.VMEM((rows, D), jnp.bfloat16),
            pltpu.VMEM((rows, LANES), jnp.float32),
            pltpu.VMEM((len(shards) * local_blocks, point_blocks, LANES), jnp.float32),
            pltpu.VMEM((2, rows, CHUNK), jnp.float32),
        ],
        compiler_params=compiler_params(),
        cost_estimate=pl.CostEstimate(
            flops=2 * rows * 2 * half * D,
            bytes_accessed=2 * half * D * 2 + rows * half * 4,
            transcendentals=rows * 2 * half,
        ),
    )(*args)


def write_message(out, total_ref, mass):
    size = total_ref.shape[0]
    for j in range(D // LANES):
        out[j * size : (j + 1) * size, :] = total_ref[:, j * LANES : (j + 1) * LANES].astype(
            jnp.bfloat16
        )
    coarse = mass.astype(jnp.bfloat16).astype(jnp.float32)
    out[D // LANES * size :, :] = jnp.concatenate([coarse, mass - coarse], 0).astype(jnp.bfloat16)


def merge_kernel(total_ref, mass_ref, arrived_ref, out_ref):
    size = total_ref.shape[0]
    tail = D // LANES * size
    for j in range(D // LANES):
        rows = slice(j * size, (j + 1) * size)
        total = total_ref[:, j * LANES : (j + 1) * LANES] + arrived_ref[rows, :].astype(jnp.float32)
        out_ref[rows, :] = total.astype(jnp.bfloat16)
    sent = arrived_ref[tail:, :].astype(jnp.float32)
    mass = mass_ref[...] + sent[:8] + sent[8:]
    coarse = mass.astype(jnp.bfloat16).astype(jnp.float32)
    out_ref[tail:, :] = jnp.concatenate([coarse, mass - coarse], 0).astype(jnp.bfloat16)


def merged(total, mass, arrived):
    return pl.pallas_call(
        merge_kernel,
        in_specs=[VMEM] * 3,
        out_specs=VMEM,
        out_shape=jax.ShapeDtypeStruct(arrived.shape, arrived.dtype),
        compiler_params=compiler_params(),
    )(total, mass, arrived)


def moments_kernel(sources, sent, size, keep, first, *refs):
    core_ref, all_ref, own_ref, other_ref = refs[:4]
    tops, powers = refs[4:6], refs[6:8]
    outs = refs[8:-4]
    scale_ref, total_ref, mass_ref, weight_ref = refs[-4:]
    half = own_ref.shape[0]
    steps = half // CHUNK
    groups = half // LANES
    at_zero = core_ref[0] == 0

    parts = all_ref[:, : 2 * groups, :]
    top = jnp.max(parts, 0)
    lse = top + jnp.log2(jnp.sum(jnp.exp2(parts - top[None]), 0))
    here = jnp.where(at_zero, lse[:groups], lse[groups:])
    there = jnp.where(at_zero, lse[groups:], lse[:groups])
    for n, top_ref in enumerate(tops):
        scale_ref[n] = jnp.exp2(top_ref[...] - jnp.concatenate([here, there], 0))
    if first:
        outs[-1][...] = here * math.log(2.0)
    copies = all_ref.shape[0] // CORES
    lane = lax.broadcasted_iota(jnp.int32, (1, LANES), 1).astype(jnp.float32)

    def weigh(step):
        for at in range(GROUPS):
            group = step * GROUPS + at
            q = group * LANES // BLOCK
            part = (group * LANES % BLOCK) // LANES
            row = 2 * groups + q % (half // BLOCK)
            zero, one = all_ref[0, row : row + 1, :], all_ref[copies, row : row + 1, :]
            mine = q < half // BLOCK
            length = jnp.where(at_zero, zero if mine else one, one if mine else zero)
            live = jnp.where(lane + part * LANES < length, 1.0, 0.0)
            lanes = slice(group * LANES, (group + 1) * LANES)
            for n, (which, start) in enumerate(sources):
                scale = scale_ref[which, group : group + 1, :] * live
                for r in range(0, size, 64):
                    power = powers[which][start + r : start + r + 64, lanes].astype(jnp.float32)
                    weights = (power * scale).astype(jnp.bfloat16)
                    rows = slice(n * size + r, n * size + r + 64)
                    weight_ref[rows, lanes] = weights
                    if group == 0:
                        mass_ref[rows, :] = weights.astype(jnp.float32)
                    else:
                        mass_ref[rows, :] += weights.astype(jnp.float32)

    weigh(0)
    for step in range(2 * steps):
        if step + 1 < 2 * steps:
            weigh(step + 1)
        source, at = (own_ref, step) if step < steps else (other_ref, step - steps)
        part = jnp.dot(
            weight_ref[:, step * CHUNK : (step + 1) * CHUNK],
            source[at * CHUNK : (at + 1) * CHUNK, :],
            preferred_element_type=jnp.float32,
        )
        if step == 0:
            total_ref[...] = part
        else:
            total_ref[...] += part

    for out, n in zip(outs, (*sent, keep)):
        rows = slice(n * size, (n + 1) * size)
        mass = jnp.sum(jnp.transpose(mass_ref[rows, :]), 0, keepdims=True)
        mass = jnp.broadcast_to(mass, (8, size))
        if n == keep:
            out[...] = total_ref[rows, :]
            outs[len(sent) + 1][...] = mass
        else:
            write_message(out, total_ref.at[rows, :], mass)


def moments(core, everyone, points, tops, powers, sources, size, sent, keep, first):
    half = points[0].shape[0]
    rows = len(sources) * size
    groups = 2 * half // LANES
    message = (D // LANES * size + 16, LANES)
    out_shape = [jax.ShapeDtypeStruct(message, jnp.bfloat16)] * len(sent)
    out_shape += [
        jax.ShapeDtypeStruct((size, D), jnp.float32),
        jax.ShapeDtypeStruct((8, size), jnp.float32),
    ]
    if first:
        out_shape += [jax.ShapeDtypeStruct((half // LANES, LANES), jnp.float32)]

    def kernel(*refs):
        moments_kernel(sources, sent, size, keep, first, *refs)

    return pl.pallas_call(
        kernel,
        in_specs=[SMEM] + [VMEM] * 7,
        out_specs=[VMEM] * len(out_shape),
        out_shape=out_shape,
        scratch_shapes=[
            pltpu.VMEM((len(tops), groups, LANES), jnp.float32),
            pltpu.VMEM((rows, D), jnp.float32),
            pltpu.VMEM((rows, LANES), jnp.float32),
            pltpu.VMEM((rows, 2 * half), jnp.bfloat16),
        ],
        compiler_params=compiler_params(),
        cost_estimate=pl.CostEstimate(
            flops=2 * rows * 2 * half * D,
            bytes_accessed=2 * half * D * 2 + rows * half * 4,
            transcendentals=0,
        ),
    )(core, everyone, *points, *tops, *powers)


def finish_kernel(*refs):
    home_ref, home_mass_ref, centre_ref = refs[:3]
    arrived = refs[3:-2]
    updated_ref, mass_out_ref = refs[-2:]
    size = centre_ref.shape[0]
    tail = D // LANES * size
    mass = home_mass_ref[...]
    for message in arrived:
        sent = message[tail:, :].astype(jnp.float32)
        mass += sent[:8] + sent[8:]
    rows, width = mass_out_ref.shape
    for n in range(rows):
        mass_out_ref[n : n + 1, :] = mass[:1, n * width : (n + 1) * width]
    inverse = 1.0 / (mass[:1] + prior_mass)
    inverse = jnp.transpose(jnp.broadcast_to(inverse, (LANES, size)))
    for j in range(D // LANES):
        lanes = slice(j * LANES, (j + 1) * LANES)
        total = home_ref[:, lanes] + prior_mass * centre_ref[:, lanes].astype(jnp.float32)
        for message in arrived:
            total += message[j * size : (j + 1) * size, :].astype(jnp.float32)
        updated_ref[:, lanes] = (total * inverse).astype(jnp.bfloat16)


def finish(home, home_mass, centre, arrived, local_blocks):
    size = centre.shape[0]
    return pl.pallas_call(
        finish_kernel,
        in_specs=[VMEM] * (3 + len(arrived)),
        out_specs=[VMEM] * 2,
        out_shape=[
            jax.ShapeDtypeStruct((size, D), jnp.bfloat16),
            jax.ShapeDtypeStruct((local_blocks, size // local_blocks), jnp.float32),
        ],
        compiler_params=compiler_params(),
    )(home, home_mass, centre, *arrived)


def local(points, lengths, candidates, centroids):
    chips = lax.axis_size("chip")
    copies = CORES * lax.axis_size("cen")
    chip = lax.axis_index("chip").astype(jnp.int32).reshape(1)
    core = lax.axis_index("core").astype(jnp.int32).reshape(1)
    local_blocks, centre_rows, _ = centroids.shape
    size = local_blocks * centre_rows

    def moved(value, step):
        return lax.ppermute(value, "chip", [(c, step(c) % chips) for c in range(chips)])

    def ahead(c):
        return c + 1

    def back(c):
        return c - 1

    def across(c):
        return c // ROW * ROW + (c + ROW // 2) % ROW

    def outward(c):
        return c + ROW if c % ROW < ROW // 2 else c - ROW

    def inward(c):
        return c - ROW if c % ROW < ROW // 2 else c + ROW

    def swapped(value):
        return lax.ppermute(value, "core", [(0, 1), (1, 0)])

    centre = centroids.reshape(size, D)
    row = moved(centre, across)
    near = [moved(centre, ahead), moved(centre, back)]
    beyond = moved(row, outward)
    other = swapped(points)
    candidates = lax.all_gather(candidates, "core")

    first_power, first_max, first_sum, kept = score(
        ("row", "own"),
        chips,
        chip,
        core,
        candidates,
        [pltpu.with_memory_space_constraint(points, pltpu.HBM), other],
        [row, pltpu.with_memory_space_constraint(centre, pltpu.HBM)],
        local_blocks,
    )
    points = [kept, other]
    last_power, last_max, message = score(
        ("before", "after", "beyond"),
        chips,
        chip,
        core,
        candidates,
        points,
        [*near, beyond],
        local_blocks,
        ((first_max, first_sum), lengths, copies),
    )
    everyone = lax.all_to_all(message, ("core", "cen"), 0, 0)
    tops, powers = (first_max, last_max), (first_power, last_power)
    beyond, row, row_mass, lse = moments(
        core, everyone, points, tops, powers, ((1, 2 * size), (0, 0)), size, (0,), 1, True
    )
    beyond = moved(beyond, inward)
    before, after, home, home_mass = moments(
        core, everyone, points, tops, powers, ((1, 0), (1, size), (0, size)), size, (0, 1), 2, False
    )
    arrived = [moved(after, ahead), moved(before, back)]
    arrived += [moved(merged(row, row_mass, beyond), across)]
    updated, masses = finish(home, home_mass, centre, arrived, local_blocks)
    return updated.reshape(centroids.shape), masses, lse.reshape(-1)


def solution(mesh):
    pt, cen = mesh.axis_names
    split = Mesh(
        mesh.devices.reshape(mesh.shape[pt] // CORES, CORES, mesh.shape[cen]),
        ("chip", "core", "cen"),
    )
    whole_pt = ("chip", "core")
    return jax.shard_map(
        local,
        mesh=split,
        in_specs=(P(whole_pt, None), P(whole_pt), P(whole_pt, None), P(whole_pt, "cen", None)),
        out_specs=(P(whole_pt, "cen", None), P(whole_pt, "cen"), P(whole_pt)),
        check_vma=False,
    )
```

```python
import math

import jax
import jax.numpy as jnp
from jax import lax
from jax.experimental import pallas as pl
from jax.experimental.pallas import tpu as pltpu
from jax.sharding import Mesh
from jax.sharding import PartitionSpec as P

D = 1024
CORES = 2
ROW = 4
BLOCK = 256
LANES = 128
CHUNK = 512
GROUPS = CHUNK // LANES
FAR = -1e30
VMEM_LIMIT = 24 << 20

sharpness_factor = 1.5
prior_mass = 1.0
SHARP = sharpness_factor * math.sqrt(D) / math.log(2.0)

SMEM = pl.BlockSpec(memory_space=pltpu.SMEM)
VMEM = pl.BlockSpec(memory_space=pltpu.VMEM)


def compiler_params():
    return pltpu.CompilerParams(vmem_limit_bytes=VMEM_LIMIT)


def fill_rows(shards, rows_ref, square_ref, first):
    size = shards[0].shape[0]
    for n, shard in enumerate(shards, first):
        for r in range(0, size, 32):
            value = shard[r : r + 32, :]
            at = slice(n * size + r, n * size + r + 32)
            rows_ref[at, :] = value
            wide = value.astype(jnp.float32)
            squares = jnp.sum(wide * wide, 1, keepdims=True) * (-SHARP)
            square_ref[at, :] = jnp.broadcast_to(squares, (32, LANES))


def reached(name, chip, chips):
    low = lax.rem(chip, ROW) < ROW // 2
    step = {
        "before": chips - 1,
        "after": 1,
        "own": 0,
        "row": jnp.where(low, 2, chips - 2),
        "beyond": jnp.where(low, chips - 2, 2),
    }[name]
    return lax.rem(chip + step, chips)


def fill_mask(names, chips, local_blocks, chip_ref, core_ref, candidate_ref, mask_ref):
    count = candidate_ref.shape[1]
    own, other = candidate_ref[core_ref[0]], candidate_ref[1 - core_ref[0]]
    held = 0
    for name in names:
        owner = reached(name, chip_ref[0], chips) * CORES + core_ref[0]
        for n in range(local_blocks):
            block = owner * local_blocks + n
            for at, ids in ((0, own), (count, other)):
                here = jnp.where(ids == block, 0.0, FAR).astype(jnp.float32)
                here = jnp.max(here, 1, keepdims=True)
                mask_ref[held, at : at + count, :] = jnp.broadcast_to(here, (count, LANES))
            held += 1


def folded(op, tile):
    parts = [tile[r : r + 8] for r in range(0, tile.shape[0], 8)]
    while len(parts) > 1:
        parts = [op(a, b) for a, b in zip(parts[::2], parts[1::2])]
    return parts[0]


def score_kernel(names, chips, local_blocks, later, *refs):
    chip_ref, core_ref, candidate_ref = refs[:3]
    own_ref, other_ref = refs[3:5]
    shards = list(refs[5 : 5 + len(names)])
    rest = refs[5 + len(names) :]
    copies = []
    if later:
        early_max, early_sum, length_ref, power_ref, max_ref, message_ref = rest[:6]
        sum_ref = rest[6]
    else:
        power_ref, max_ref, sum_ref, kept_ref, centre_ref, semaphores = rest[:6]
        copies = [
            pltpu.make_async_copy(shards[-1], centre_ref, semaphores.at[0]),
            pltpu.make_async_copy(own_ref, kept_ref, semaphores.at[1]),
        ]
        own_ref, shards[-1] = kept_ref, centre_ref
    rows_ref, square_ref, mask_ref, product_ref = rest[-4:]
    half = own_ref.shape[0]
    steps = half // CHUNK
    centre_rows = shards[0].shape[0] // local_blocks
    blocks = len(names) * local_blocks

    for copy in copies:
        copy.start()
    if copies:
        fill_rows(shards[:-1], rows_ref, square_ref, 0)
        copies[0].wait()
        fill_rows(shards[-1:], rows_ref, square_ref, len(shards) - 1)
    else:
        fill_rows(shards, rows_ref, square_ref, 0)

    def multiply(step):
        source, first = (other_ref, step) if step < steps else (own_ref, step - steps)
        if step == steps and copies:
            copies[1].wait()
        product_ref[step % 2] = lax.dot_general(
            rows_ref[...],
            source[first * CHUNK : (first + 1) * CHUNK, :],
            (((1,), (1,)), ((), ())),
            preferred_element_type=jnp.float32,
        )

    multiply(0)
    fill_mask(names, chips, local_blocks, chip_ref, core_ref, candidate_ref, mask_ref)
    for step in range(2 * steps):
        if step + 1 < 2 * steps:
            multiply(step + 1)
        held = product_ref.at[step % 2]
        for n in range(GROUPS):
            lanes = slice(n * LANES, (n + 1) * LANES)
            place = (step * CHUNK + half) % (2 * half) + n * LANES
            q = place // BLOCK
            tops = []
            for b in range(blocks):
                rows = slice(b * centre_rows, (b + 1) * centre_rows)
                bias = square_ref[rows, :] + mask_ref[b, q : q + 1, :]
                logits = held[rows, lanes] * (2.0 * SHARP) + bias
                held[rows, lanes] = logits
                tops.append(folded(jnp.maximum, logits))
            top = tops[0]
            for more in tops[1:]:
                top = jnp.maximum(top, more)
            top = jnp.max(top, 0, keepdims=True)
            total = jnp.zeros((8, LANES), jnp.float32)
            for b in range(blocks):
                rows = slice(b * centre_rows, (b + 1) * centre_rows)
                power = jnp.exp2(held[rows, lanes] - top)
                total += folded(jnp.add, power)
                power_ref[rows, place : place + LANES] = power.astype(jnp.bfloat16)
            group = place // LANES
            max_ref[group : group + 1, :] = top
            sum_ref[group : group + 1, :] = jnp.sum(total, 0, keepdims=True)

    if later:
        both = jnp.maximum(max_ref[...], early_max[...])
        summed = sum_ref[...] * jnp.exp2(max_ref[...] - both)
        summed += early_sum[...] * jnp.exp2(early_max[...] - both)
        lse = both + jnp.log2(summed)
        groups = half // LANES
        here, there = lse[:groups], lse[groups:]
        first = core_ref[0] == 0
        lengths = [
            jnp.full((1, LANES), length_ref[q].astype(jnp.float32)) for q in range(half // BLOCK)
        ]
        lengths += [jnp.zeros((1, LANES), jnp.float32)] * (-len(lengths) % 8)
        message = jnp.concatenate(
            [jnp.where(first, here, there), jnp.where(first, there, here), *lengths], 0
        )
        for n in range(message_ref.shape[0]):
            message_ref[n] = message


def score(names, chips, chip, core, candidates, points, shards, local_blocks, later=None):
    size = shards[0].shape[0]
    half = points[0].shape[0]
    rows = size * len(shards)
    groups = 2 * half // LANES
    stat = jax.ShapeDtypeStruct((groups, LANES), jnp.float32)
    out_shape = [jax.ShapeDtypeStruct((rows, 2 * half), jnp.bfloat16), stat]
    scratch = []
    in_specs = [SMEM, SMEM] + [VMEM] * (3 + len(shards))
    args = [chip, core, candidates, *points, *shards]
    if later is None:
        in_specs[3] = in_specs[-1] = pl.BlockSpec(memory_space=pltpu.HBM)
        out_shape += [stat, jax.ShapeDtypeStruct(points[0].shape, points[0].dtype)]
        scratch += [pltpu.VMEM((size, D), shards[0].dtype), pltpu.SemaphoreType.DMA((2,))]
    else:
        early, lengths, copies = later
        in_specs += [VMEM, VMEM, SMEM]
        args += [*early, lengths]
        spare = -(-(half // BLOCK) // 8) * 8
        out_shape += [jax.ShapeDtypeStruct((copies, groups + spare, LANES), jnp.float32)]
        scratch += [pltpu.VMEM((groups, LANES), jnp.float32)]
    point_blocks = -(-(2 * half // BLOCK) // 8) * 8

    def kernel(*refs):
        score_kernel(names, chips, local_blocks, later is not None, *refs)

    return pl.pallas_call(
        kernel,
        in_specs=in_specs,
        out_specs=[VMEM] * len(out_shape),
        out_shape=out_shape,
        scratch_shapes=scratch
        + [
            pltpu.VMEM((rows, D), jnp.bfloat16),
            pltpu.VMEM((rows, LANES), jnp.float32),
            pltpu.VMEM((len(shards) * local_blocks, point_blocks, LANES), jnp.float32),
            pltpu.VMEM((2, rows, CHUNK), jnp.float32),
        ],
        compiler_params=compiler_params(),
        cost_estimate=pl.CostEstimate(
            flops=2 * rows * 2 * half * D,
            bytes_accessed=2 * half * D * 2 + rows * half * 4,
            transcendentals=rows * 2 * half,
        ),
    )(*args)


def write_message(out, total_ref, mass):
    size = total_ref.shape[0]
    for j in range(D // LANES):
        out[j * size : (j + 1) * size, :] = total_ref[:, j * LANES : (j + 1) * LANES].astype(
            jnp.bfloat16
        )
    coarse = mass.astype(jnp.bfloat16).astype(jnp.float32)
    out[D // LANES * size :, :] = jnp.concatenate([coarse, mass - coarse], 0).astype(jnp.bfloat16)


def merge_kernel(total_ref, mass_ref, arrived_ref, out_ref):
    size = total_ref.shape[0]
    tail = D // LANES * size
    for j in range(D // LANES):
        rows = slice(j * size, (j + 1) * size)
        total = total_ref[:, j * LANES : (j + 1) * LANES] + arrived_ref[rows, :].astype(jnp.float32)
        out_ref[rows, :] = total.astype(jnp.bfloat16)
    sent = arrived_ref[tail:, :].astype(jnp.float32)
    mass = mass_ref[...] + sent[:8] + sent[8:]
    coarse = mass.astype(jnp.bfloat16).astype(jnp.float32)
    out_ref[tail:, :] = jnp.concatenate([coarse, mass - coarse], 0).astype(jnp.bfloat16)


def merged(total, mass, arrived):
    return pl.pallas_call(
        merge_kernel,
        in_specs=[VMEM] * 3,
        out_specs=VMEM,
        out_shape=jax.ShapeDtypeStruct(arrived.shape, arrived.dtype),
        compiler_params=compiler_params(),
    )(total, mass, arrived)


def moments_kernel(sources, sent, size, keep, first, *refs):
    core_ref, all_ref, own_ref, other_ref = refs[:4]
    tops, powers = refs[4:6], refs[6:8]
    outs = refs[8:-4]
    scale_ref, total_ref, mass_ref, weight_ref = refs[-4:]
    half = own_ref.shape[0]
    steps = half // CHUNK
    groups = half // LANES
    at_zero = core_ref[0] == 0

    parts = all_ref[:, : 2 * groups, :]
    top = jnp.max(parts, 0)
    lse = top + jnp.log2(jnp.sum(jnp.exp2(parts - top[None]), 0))
    here = jnp.where(at_zero, lse[:groups], lse[groups:])
    there = jnp.where(at_zero, lse[groups:], lse[:groups])
    for n, top_ref in enumerate(tops):
        scale_ref[n] = jnp.exp2(top_ref[...] - jnp.concatenate([here, there], 0))
    if first:
        outs[-1][...] = here * math.log(2.0)
    copies = all_ref.shape[0] // CORES
    lane = lax.broadcasted_iota(jnp.int32, (1, LANES), 1).astype(jnp.float32)

    def weigh(step):
        for at in range(GROUPS):
            group = step * GROUPS + at
            q = group * LANES // BLOCK
            part = (group * LANES % BLOCK) // LANES
            row = 2 * groups + q % (half // BLOCK)
            zero, one = all_ref[0, row : row + 1, :], all_ref[copies, row : row + 1, :]
            mine = q < half // BLOCK
            length = jnp.where(at_zero, zero if mine else one, one if mine else zero)
            live = jnp.where(lane + part * LANES < length, 1.0, 0.0)
            lanes = slice(group * LANES, (group + 1) * LANES)
            for n, (which, start) in enumerate(sources):
                scale = scale_ref[which, group : group + 1, :] * live
                for r in range(0, size, 64):
                    power = powers[which][start + r : start + r + 64, lanes].astype(jnp.float32)
                    weights = (power * scale).astype(jnp.bfloat16)
                    rows = slice(n * size + r, n * size + r + 64)
                    weight_ref[rows, lanes] = weights
                    if group == 0:
                        mass_ref[rows, :] = weights.astype(jnp.float32)
                    else:
                        mass_ref[rows, :] += weights.astype(jnp.float32)

    weigh(0)
    for step in range(2 * steps):
        if step + 1 < 2 * steps:
            weigh(step + 1)
        source, at = (own_ref, step) if step < steps else (other_ref, step - steps)
        part = jnp.dot(
            weight_ref[:, step * CHUNK : (step + 1) * CHUNK],
            source[at * CHUNK : (at + 1) * CHUNK, :],
            preferred_element_type=jnp.float32,
        )
        if step == 0:
            total_ref[...] = part
        else:
            total_ref[...] += part

    for out, n in zip(outs, sent if keep is None else (*sent, keep)):
        rows = slice(n * size, (n + 1) * size)
        mass = jnp.sum(jnp.transpose(mass_ref[rows, :]), 0, keepdims=True)
        mass = jnp.broadcast_to(mass, (8, size))
        if n == keep:
            out[...] = total_ref[rows, :]
            outs[len(sent) + 1][...] = mass
        else:
            write_message(out, total_ref.at[rows, :], mass)


def moments(core, everyone, points, tops, powers, sources, size, sent, keep, first):
    half = points[0].shape[0]
    rows = len(sources) * size
    groups = 2 * half // LANES
    message = (D // LANES * size + 16, LANES)
    out_shape = [jax.ShapeDtypeStruct(message, jnp.bfloat16)] * len(sent)
    if keep is not None:
        out_shape += [
            jax.ShapeDtypeStruct((size, D), jnp.float32),
            jax.ShapeDtypeStruct((8, size), jnp.float32),
        ]
    if first:
        out_shape += [jax.ShapeDtypeStruct((half // LANES, LANES), jnp.float32)]

    def kernel(*refs):
        moments_kernel(sources, sent, size, keep, first, *refs)

    return pl.pallas_call(
        kernel,
        in_specs=[SMEM] + [VMEM] * 7,
        out_specs=[VMEM] * len(out_shape),
        out_shape=out_shape,
        scratch_shapes=[
            pltpu.VMEM((len(tops), groups, LANES), jnp.float32),
            pltpu.VMEM((rows, D), jnp.float32),
            pltpu.VMEM((rows, LANES), jnp.float32),
            pltpu.VMEM((rows, 2 * half), jnp.bfloat16),
        ],
        compiler_params=compiler_params(),
        cost_estimate=pl.CostEstimate(
            flops=2 * rows * 2 * half * D,
            bytes_accessed=2 * half * D * 2 + rows * half * 4,
            transcendentals=0,
        ),
    )(core, everyone, *points, *tops, *powers)


def finish_kernel(*refs):
    home_ref, home_mass_ref, centre_ref = refs[:3]
    arrived = refs[3:-2]
    updated_ref, mass_out_ref = refs[-2:]
    size = centre_ref.shape[0]
    tail = D // LANES * size
    mass = home_mass_ref[...]
    for message in arrived:
        sent = message[tail:, :].astype(jnp.float32)
        mass += sent[:8] + sent[8:]
    rows, width = mass_out_ref.shape
    for n in range(rows):
        mass_out_ref[n : n + 1, :] = mass[:1, n * width : (n + 1) * width]
    inverse = 1.0 / (mass[:1] + prior_mass)
    inverse = jnp.transpose(jnp.broadcast_to(inverse, (LANES, size)))
    for j in range(D // LANES):
        lanes = slice(j * LANES, (j + 1) * LANES)
        total = home_ref[:, lanes] + prior_mass * centre_ref[:, lanes].astype(jnp.float32)
        for message in arrived:
            total += message[j * size : (j + 1) * size, :].astype(jnp.float32)
        updated_ref[:, lanes] = (total * inverse).astype(jnp.bfloat16)


def finish(home, home_mass, centre, arrived, local_blocks):
    size = centre.shape[0]
    return pl.pallas_call(
        finish_kernel,
        in_specs=[VMEM] * (3 + len(arrived)),
        out_specs=[VMEM] * 2,
        out_shape=[
            jax.ShapeDtypeStruct((size, D), jnp.bfloat16),
            jax.ShapeDtypeStruct((local_blocks, size // local_blocks), jnp.float32),
        ],
        compiler_params=compiler_params(),
    )(home, home_mass, centre, *arrived)


def local(points, lengths, candidates, centroids):
    chips = lax.axis_size("chip")
    copies = CORES * lax.axis_size("cen")
    chip = lax.axis_index("chip").astype(jnp.int32).reshape(1)
    core = lax.axis_index("core").astype(jnp.int32).reshape(1)
    local_blocks, centre_rows, _ = centroids.shape
    size = local_blocks * centre_rows

    def moved(value, step):
        return lax.ppermute(value, "chip", [(c, step(c) % chips) for c in range(chips)])

    def ahead(c):
        return c + 1

    def back(c):
        return c - 1

    def across(c):
        return c // ROW * ROW + (c + ROW // 2) % ROW

    def outward(c):
        return c + ROW if c % ROW < ROW // 2 else c - ROW

    def inward(c):
        return c - ROW if c % ROW < ROW // 2 else c + ROW

    def swapped(value):
        return lax.ppermute(value, "core", [(0, 1), (1, 0)])

    centre = centroids.reshape(size, D)
    row = moved(centre, across)
    near = [moved(centre, ahead), moved(centre, back)]
    beyond = moved(row, outward)
    other = swapped(points)
    candidates = lax.all_gather(candidates, "core")

    first_power, first_max, first_sum, kept = score(
        ("row", "before", "own"),
        chips,
        chip,
        core,
        candidates,
        [pltpu.with_memory_space_constraint(points, pltpu.HBM), other],
        [row, near[0], pltpu.with_memory_space_constraint(centre, pltpu.HBM)],
        local_blocks,
    )
    points = [kept, other]
    last_power, last_max, message = score(
        ("after", "beyond"),
        chips,
        chip,
        core,
        candidates,
        points,
        [near[1], beyond],
        local_blocks,
        ((first_max, first_sum), lengths, copies),
    )
    everyone = lax.all_to_all(message, ("core", "cen"), 0, 0)
    tops, powers = (first_max, last_max), (first_power, last_power)
    beyond, lse = moments(
        core, everyone, points, tops, powers, ((1, size),), size, (0,), None, True
    )
    beyond = moved(beyond, inward)
    before, after, row, row_mass = moments(
        core, everyone, points, tops, powers, ((0, size), (1, 0), (0, 0)), size, (0, 1), 2, False
    )
    arrived = [moved(after, ahead), moved(before, back)]
    arrived += [moved(merged(row, row_mass, beyond), across)]
    home, home_mass = moments(
        core, everyone, points, tops, powers, ((0, 2 * size),), size, (), 0, False
    )
    updated, masses = finish(home, home_mass, centre, arrived, local_blocks)
    return updated.reshape(centroids.shape), masses, lse.reshape(-1)


def solution(mesh):
    pt, cen = mesh.axis_names
    split = Mesh(
        mesh.devices.reshape(mesh.shape[pt] // CORES, CORES, mesh.shape[cen]),
        ("chip", "core", "cen"),
    )
    whole_pt = ("chip", "core")
    return jax.shard_map(
        local,
        mesh=split,
        in_specs=(P(whole_pt, None), P(whole_pt), P(whole_pt, None), P(whole_pt, "cen", None)),
        out_specs=(P(whole_pt, "cen", None), P(whole_pt, "cen"), P(whole_pt)),
        check_vma=False,
    )
```

```python
import math

import jax
import jax.numpy as jnp
from jax import lax
from jax.experimental import pallas as pl
from jax.experimental.pallas import tpu as pltpu
from jax.sharding import Mesh
from jax.sharding import PartitionSpec as P

D = 1024
CORES = 2
ROW = 4
BLOCK = 256
LANES = 128
CHUNK = 512
GROUPS = CHUNK // LANES
FAR = -1e30
VMEM_LIMIT = 24 << 20

sharpness_factor = 1.5
prior_mass = 1.0
SHARP = sharpness_factor * math.sqrt(D) / math.log(2.0)

SMEM = pl.BlockSpec(memory_space=pltpu.SMEM)
VMEM = pl.BlockSpec(memory_space=pltpu.VMEM)


def compiler_params():
    return pltpu.CompilerParams(vmem_limit_bytes=VMEM_LIMIT)


def fill_rows(shards, rows_ref, square_ref, first):
    size = shards[0].shape[0]
    for n, shard in enumerate(shards, first):
        for r in range(0, size, 32):
            value = shard[r : r + 32, :]
            at = slice(n * size + r, n * size + r + 32)
            rows_ref[at, :] = value
            wide = value.astype(jnp.float32)
            squares = jnp.sum(wide * wide, 1, keepdims=True) * (-SHARP)
            square_ref[at, :] = jnp.broadcast_to(squares, (32, LANES))


def reached(name, chip, chips):
    low = lax.rem(chip, ROW) < ROW // 2
    step = {
        "before": chips - 1,
        "after": 1,
        "own": 0,
        "row": jnp.where(low, 2, chips - 2),
        "beyond": jnp.where(low, chips - 2, 2),
    }[name]
    return lax.rem(chip + step, chips)


def fill_mask(names, chips, local_blocks, chip_ref, core_ref, candidate_ref, mask_ref):
    count = candidate_ref.shape[1]
    own, other = candidate_ref[core_ref[0]], candidate_ref[1 - core_ref[0]]
    held = 0
    for name in names:
        owner = reached(name, chip_ref[0], chips) * CORES + core_ref[0]
        for n in range(local_blocks):
            block = owner * local_blocks + n
            for at, ids in ((0, own), (count, other)):
                here = jnp.where(ids == block, 0.0, FAR).astype(jnp.float32)
                here = jnp.max(here, 1, keepdims=True)
                mask_ref[held, at : at + count, :] = jnp.broadcast_to(here, (count, LANES))
            held += 1


def folded(op, tile):
    parts = [tile[r : r + 8] for r in range(0, tile.shape[0], 8)]
    while len(parts) > 1:
        parts = [op(a, b) for a, b in zip(parts[::2], parts[1::2])]
    return parts[0]


def score_kernel(names, chips, local_blocks, later, *refs):
    chip_ref, core_ref, candidate_ref = refs[:3]
    own_ref, other_ref = refs[3:5]
    shards = list(refs[5 : 5 + len(names)])
    rest = refs[5 + len(names) :]
    copies = []
    if later:
        early_max, early_sum, length_ref, power_ref, max_ref, message_ref = rest[:6]
        sum_ref = rest[6]
    else:
        power_ref, max_ref, sum_ref, kept_ref, centre_ref, semaphores = rest[:6]
        copies = [
            pltpu.make_async_copy(shards[-1], centre_ref, semaphores.at[0]),
            pltpu.make_async_copy(own_ref, kept_ref, semaphores.at[1]),
        ]
        own_ref, shards[-1] = kept_ref, centre_ref
    rows_ref, square_ref, mask_ref, product_ref = rest[-4:]
    half = own_ref.shape[0]
    steps = half // CHUNK
    centre_rows = shards[0].shape[0] // local_blocks
    blocks = len(names) * local_blocks

    for copy in copies:
        copy.start()
    if copies:
        fill_rows(shards[:-1], rows_ref, square_ref, 0)
        copies[0].wait()
        fill_rows(shards[-1:], rows_ref, square_ref, len(shards) - 1)
    else:
        fill_rows(shards, rows_ref, square_ref, 0)

    def multiply(step):
        source, first = (other_ref, step) if step < steps else (own_ref, step - steps)
        if step == steps and copies:
            copies[1].wait()
        product_ref[step % 2] = lax.dot_general(
            rows_ref[...],
            source[first * CHUNK : (first + 1) * CHUNK, :],
            (((1,), (1,)), ((), ())),
            preferred_element_type=jnp.float32,
        )

    multiply(0)
    fill_mask(names, chips, local_blocks, chip_ref, core_ref, candidate_ref, mask_ref)
    for step in range(2 * steps):
        if step + 1 < 2 * steps:
            multiply(step + 1)
        held = product_ref.at[step % 2]
        for n in range(GROUPS):
            lanes = slice(n * LANES, (n + 1) * LANES)
            place = (step * CHUNK + half) % (2 * half) + n * LANES
            q = place // BLOCK
            tops = []
            for b in range(blocks):
                rows = slice(b * centre_rows, (b + 1) * centre_rows)
                bias = square_ref[rows, :] + mask_ref[b, q : q + 1, :]
                logits = held[rows, lanes] * (2.0 * SHARP) + bias
                held[rows, lanes] = logits
                tops.append(folded(jnp.maximum, logits))
            top = tops[0]
            for more in tops[1:]:
                top = jnp.maximum(top, more)
            top = jnp.max(top, 0, keepdims=True)
            total = jnp.zeros((8, LANES), jnp.float32)
            for b in range(blocks):
                rows = slice(b * centre_rows, (b + 1) * centre_rows)
                power = jnp.exp2(held[rows, lanes] - top)
                total += folded(jnp.add, power)
                power_ref[rows, place : place + LANES] = power.astype(jnp.bfloat16)
            group = place // LANES
            max_ref[group : group + 1, :] = top
            sum_ref[group : group + 1, :] = jnp.sum(total, 0, keepdims=True)

    if later:
        both = jnp.maximum(max_ref[...], early_max[...])
        summed = sum_ref[...] * jnp.exp2(max_ref[...] - both)
        summed += early_sum[...] * jnp.exp2(early_max[...] - both)
        lse = both + jnp.log2(summed)
        groups = half // LANES
        here, there = lse[:groups], lse[groups:]
        first = core_ref[0] == 0
        lengths = [
            jnp.full((1, LANES), length_ref[q].astype(jnp.float32)) for q in range(half // BLOCK)
        ]
        lengths += [jnp.zeros((1, LANES), jnp.float32)] * (-len(lengths) % 8)
        message = jnp.concatenate(
            [jnp.where(first, here, there), jnp.where(first, there, here), *lengths], 0
        )
        for n in range(message_ref.shape[0]):
            message_ref[n] = message


def score(names, chips, chip, core, candidates, points, shards, local_blocks, later=None):
    size = shards[0].shape[0]
    half = points[0].shape[0]
    rows = size * len(shards)
    groups = 2 * half // LANES
    stat = jax.ShapeDtypeStruct((groups, LANES), jnp.float32)
    out_shape = [jax.ShapeDtypeStruct((rows, 2 * half), jnp.bfloat16), stat]
    scratch = []
    in_specs = [SMEM, SMEM] + [VMEM] * (3 + len(shards))
    args = [chip, core, candidates, *points, *shards]
    if later is None:
        in_specs[3] = in_specs[-1] = pl.BlockSpec(memory_space=pltpu.HBM)
        out_shape += [stat, jax.ShapeDtypeStruct(points[0].shape, points[0].dtype)]
        scratch += [pltpu.VMEM((size, D), shards[0].dtype), pltpu.SemaphoreType.DMA((2,))]
    else:
        early, lengths, copies = later
        in_specs += [VMEM, VMEM, SMEM]
        args += [*early, lengths]
        spare = -(-(half // BLOCK) // 8) * 8
        out_shape += [jax.ShapeDtypeStruct((copies, groups + spare, LANES), jnp.float32)]
        scratch += [pltpu.VMEM((groups, LANES), jnp.float32)]
    point_blocks = -(-(2 * half // BLOCK) // 8) * 8

    def kernel(*refs):
        score_kernel(names, chips, local_blocks, later is not None, *refs)

    return pl.pallas_call(
        kernel,
        in_specs=in_specs,
        out_specs=[VMEM] * len(out_shape),
        out_shape=out_shape,
        scratch_shapes=scratch
        + [
            pltpu.VMEM((rows, D), jnp.bfloat16),
            pltpu.VMEM((rows, LANES), jnp.float32),
            pltpu.VMEM((len(shards) * local_blocks, point_blocks, LANES), jnp.float32),
            pltpu.VMEM((2, rows, CHUNK), jnp.float32),
        ],
        compiler_params=compiler_params(),
        cost_estimate=pl.CostEstimate(
            flops=2 * rows * 2 * half * D,
            bytes_accessed=2 * half * D * 2 + rows * half * 4,
            transcendentals=rows * 2 * half,
        ),
    )(*args)


def write_message(out, total_ref, mass):
    size = total_ref.shape[0]
    for j in range(D // LANES):
        out[j * size : (j + 1) * size, :] = total_ref[:, j * LANES : (j + 1) * LANES].astype(
            jnp.bfloat16
        )
    coarse = mass.astype(jnp.bfloat16).astype(jnp.float32)
    out[D // LANES * size :, :] = jnp.concatenate([coarse, mass - coarse], 0).astype(jnp.bfloat16)


def merge_kernel(total_ref, mass_ref, arrived_ref, out_ref):
    size = total_ref.shape[0]
    tail = D // LANES * size
    for j in range(D // LANES):
        rows = slice(j * size, (j + 1) * size)
        total = total_ref[:, j * LANES : (j + 1) * LANES] + arrived_ref[rows, :].astype(jnp.float32)
        out_ref[rows, :] = total.astype(jnp.bfloat16)
    sent = arrived_ref[tail:, :].astype(jnp.float32)
    mass = mass_ref[...] + sent[:8] + sent[8:]
    coarse = mass.astype(jnp.bfloat16).astype(jnp.float32)
    out_ref[tail:, :] = jnp.concatenate([coarse, mass - coarse], 0).astype(jnp.bfloat16)


def merged(total, mass, arrived):
    return pl.pallas_call(
        merge_kernel,
        in_specs=[VMEM] * 3,
        out_specs=VMEM,
        out_shape=jax.ShapeDtypeStruct(arrived.shape, arrived.dtype),
        compiler_params=compiler_params(),
    )(total, mass, arrived)


def moments_kernel(sources, sent, size, keep, first, *refs):
    core_ref, all_ref, own_ref, other_ref = refs[:4]
    tops, powers = refs[4:6], refs[6:8]
    outs = refs[8:-4]
    scale_ref, total_ref, mass_ref, weight_ref = refs[-4:]
    half = own_ref.shape[0]
    steps = half // CHUNK
    groups = half // LANES
    at_zero = core_ref[0] == 0

    parts = all_ref[:, : 2 * groups, :]
    top = jnp.max(parts, 0)
    lse = top + jnp.log2(jnp.sum(jnp.exp2(parts - top[None]), 0))
    here = jnp.where(at_zero, lse[:groups], lse[groups:])
    there = jnp.where(at_zero, lse[groups:], lse[:groups])
    for n, top_ref in enumerate(tops):
        scale_ref[n] = jnp.exp2(top_ref[...] - jnp.concatenate([here, there], 0))
    if first:
        outs[-1][...] = here * math.log(2.0)
    copies = all_ref.shape[0] // CORES
    lane = lax.broadcasted_iota(jnp.int32, (1, LANES), 1).astype(jnp.float32)

    def weigh(step):
        for at in range(GROUPS):
            group = step * GROUPS + at
            q = group * LANES // BLOCK
            part = (group * LANES % BLOCK) // LANES
            row = 2 * groups + q % (half // BLOCK)
            zero, one = all_ref[0, row : row + 1, :], all_ref[copies, row : row + 1, :]
            mine = q < half // BLOCK
            length = jnp.where(at_zero, zero if mine else one, one if mine else zero)
            live = jnp.where(lane + part * LANES < length, 1.0, 0.0)
            lanes = slice(group * LANES, (group + 1) * LANES)
            for n, (which, start) in enumerate(sources):
                scale = scale_ref[which, group : group + 1, :] * live
                for r in range(0, size, 64):
                    power = powers[which][start + r : start + r + 64, lanes].astype(jnp.float32)
                    weights = (power * scale).astype(jnp.bfloat16)
                    rows = slice(n * size + r, n * size + r + 64)
                    weight_ref[rows, lanes] = weights
                    if group == 0:
                        mass_ref[rows, :] = weights.astype(jnp.float32)
                    else:
                        mass_ref[rows, :] += weights.astype(jnp.float32)

    weigh(0)
    for step in range(2 * steps):
        if step + 1 < 2 * steps:
            weigh(step + 1)
        source, at = (own_ref, step) if step < steps else (other_ref, step - steps)
        part = jnp.dot(
            weight_ref[:, step * CHUNK : (step + 1) * CHUNK],
            source[at * CHUNK : (at + 1) * CHUNK, :],
            preferred_element_type=jnp.float32,
        )
        if step == 0:
            total_ref[...] = part
        else:
            total_ref[...] += part

    for out, n in zip(outs, sent if keep is None else (*sent, keep)):
        rows = slice(n * size, (n + 1) * size)
        mass = jnp.sum(jnp.transpose(mass_ref[rows, :]), 0, keepdims=True)
        mass = jnp.broadcast_to(mass, (8, size))
        if n == keep:
            out[...] = total_ref[rows, :]
            outs[len(sent) + 1][...] = mass
        else:
            write_message(out, total_ref.at[rows, :], mass)


def moments(core, everyone, points, tops, powers, sources, size, sent, keep, first):
    half = points[0].shape[0]
    rows = len(sources) * size
    groups = 2 * half // LANES
    message = (D // LANES * size + 16, LANES)
    out_shape = [jax.ShapeDtypeStruct(message, jnp.bfloat16)] * len(sent)
    if keep is not None:
        out_shape += [
            jax.ShapeDtypeStruct((size, D), jnp.float32),
            jax.ShapeDtypeStruct((8, size), jnp.float32),
        ]
    if first:
        out_shape += [jax.ShapeDtypeStruct((half // LANES, LANES), jnp.float32)]

    def kernel(*refs):
        moments_kernel(sources, sent, size, keep, first, *refs)

    return pl.pallas_call(
        kernel,
        in_specs=[SMEM] + [VMEM] * 7,
        out_specs=[VMEM] * len(out_shape),
        out_shape=out_shape,
        scratch_shapes=[
            pltpu.VMEM((len(tops), groups, LANES), jnp.float32),
            pltpu.VMEM((rows, D), jnp.float32),
            pltpu.VMEM((rows, LANES), jnp.float32),
            pltpu.VMEM((rows, 2 * half), jnp.bfloat16),
        ],
        compiler_params=compiler_params(),
        cost_estimate=pl.CostEstimate(
            flops=2 * rows * 2 * half * D,
            bytes_accessed=2 * half * D * 2 + rows * half * 4,
            transcendentals=0,
        ),
    )(core, everyone, *points, *tops, *powers)


def finish_kernel(*refs):
    home_ref, home_mass_ref, centre_ref = refs[:3]
    arrived = refs[3:-2]
    updated_ref, mass_out_ref = refs[-2:]
    size = centre_ref.shape[0]
    tail = D // LANES * size
    mass = home_mass_ref[...]
    for message in arrived:
        sent = message[tail:, :].astype(jnp.float32)
        mass += sent[:8] + sent[8:]
    rows, width = mass_out_ref.shape
    for n in range(rows):
        mass_out_ref[n : n + 1, :] = mass[:1, n * width : (n + 1) * width]
    inverse = 1.0 / (mass[:1] + prior_mass)
    inverse = jnp.transpose(jnp.broadcast_to(inverse, (LANES, size)))
    for j in range(D // LANES):
        lanes = slice(j * LANES, (j + 1) * LANES)
        total = home_ref[:, lanes] + prior_mass * centre_ref[:, lanes].astype(jnp.float32)
        for message in arrived:
            total += message[j * size : (j + 1) * size, :].astype(jnp.float32)
        updated_ref[:, lanes] = (total * inverse).astype(jnp.bfloat16)


def finish(home, home_mass, centre, arrived, local_blocks):
    size = centre.shape[0]
    return pl.pallas_call(
        finish_kernel,
        in_specs=[VMEM] * (3 + len(arrived)),
        out_specs=[VMEM] * 2,
        out_shape=[
            jax.ShapeDtypeStruct((size, D), jnp.bfloat16),
            jax.ShapeDtypeStruct((local_blocks, size // local_blocks), jnp.float32),
        ],
        compiler_params=compiler_params(),
    )(home, home_mass, centre, *arrived)


def local(points, lengths, candidates, centroids):
    chips = lax.axis_size("chip")
    copies = CORES * lax.axis_size("cen")
    chip = lax.axis_index("chip").astype(jnp.int32).reshape(1)
    core = lax.axis_index("core").astype(jnp.int32).reshape(1)
    local_blocks, centre_rows, _ = centroids.shape
    size = local_blocks * centre_rows

    def moved(value, step):
        return lax.ppermute(value, "chip", [(c, step(c) % chips) for c in range(chips)])

    def ahead(c):
        return c + 1

    def back(c):
        return c - 1

    def across(c):
        return c // ROW * ROW + (c + ROW // 2) % ROW

    def outward(c):
        return c + ROW if c % ROW < ROW // 2 else c - ROW

    def inward(c):
        return c - ROW if c % ROW < ROW // 2 else c + ROW

    def swapped(value):
        return lax.ppermute(value, "core", [(0, 1), (1, 0)])

    centre = centroids.reshape(size, D)
    row = moved(centre, across)
    near = [moved(centre, back), moved(centre, ahead)]
    beyond = moved(row, outward)
    other = swapped(points)
    candidates = lax.all_gather(candidates, "core")

    first_power, first_max, first_sum, kept = score(
        ("row", "own"),
        chips,
        chip,
        core,
        candidates,
        [pltpu.with_memory_space_constraint(points, pltpu.HBM), other],
        [row, pltpu.with_memory_space_constraint(centre, pltpu.HBM)],
        local_blocks,
    )
    points = [kept, other]
    last_power, last_max, message = score(
        ("after", "before", "beyond"),
        chips,
        chip,
        core,
        candidates,
        points,
        [*near, beyond],
        local_blocks,
        ((first_max, first_sum), lengths, copies),
    )
    everyone = lax.all_to_all(message, ("core", "cen"), 0, 0)
    tops, powers = (first_max, last_max), (first_power, last_power)
    beyond, lse = moments(
        core, everyone, points, tops, powers, ((1, 2 * size),), size, (0,), None, True
    )
    beyond = moved(beyond, inward)
    after, before, row, row_mass = moments(
        core, everyone, points, tops, powers, ((1, 0), (1, size), (0, 0)), size, (0, 1), 2, False
    )
    arrived = [moved(after, ahead), moved(before, back)]
    arrived += [moved(merged(row, row_mass, beyond), across)]
    home, home_mass = moments(
        core, everyone, points, tops, powers, ((0, size),), size, (), 0, False
    )
    updated, masses = finish(home, home_mass, centre, arrived, local_blocks)
    return updated.reshape(centroids.shape), masses, lse.reshape(-1)


def solution(mesh):
    pt, cen = mesh.axis_names
    split = Mesh(
        mesh.devices.reshape(mesh.shape[pt] // CORES, CORES, mesh.shape[cen]),
        ("chip", "core", "cen"),
    )
    whole_pt = ("chip", "core")
    return jax.shard_map(
        local,
        mesh=split,
        in_specs=(P(whole_pt, None), P(whole_pt), P(whole_pt, None), P(whole_pt, "cen", None)),
        out_specs=(P(whole_pt, "cen", None), P(whole_pt, "cen"), P(whole_pt)),
        check_vma=False,
    )
```

```python
import math

import jax
import jax.numpy as jnp
from jax import lax
from jax.experimental import pallas as pl
from jax.experimental.pallas import tpu as pltpu
from jax.sharding import Mesh
from jax.sharding import PartitionSpec as P

D = 1024
CORES = 2
ROW = 4
BLOCK = 256
LANES = 128
CHUNK = 512
GROUPS = CHUNK // LANES
FAR = -1e30
VMEM_LIMIT = 24 << 20

sharpness_factor = 1.5
prior_mass = 1.0
SHARP = sharpness_factor * math.sqrt(D) / math.log(2.0)

SMEM = pl.BlockSpec(memory_space=pltpu.SMEM)
VMEM = pl.BlockSpec(memory_space=pltpu.VMEM)


def compiler_params():
    return pltpu.CompilerParams(vmem_limit_bytes=VMEM_LIMIT)


def fill_rows(shards, rows_ref, square_ref, first):
    size = shards[0].shape[0]
    for n, shard in enumerate(shards, first):
        for r in range(0, size, 32):
            value = shard[r : r + 32, :]
            at = slice(n * size + r, n * size + r + 32)
            rows_ref[at, :] = value
            wide = value.astype(jnp.float32)
            squares = jnp.sum(wide * wide, 1, keepdims=True) * (-SHARP)
            square_ref[at, :] = jnp.broadcast_to(squares, (32, LANES))


def reached(name, chip, chips):
    low = lax.rem(chip, ROW) < ROW // 2
    step = {
        "before": chips - 1,
        "after": 1,
        "own": 0,
        "row": jnp.where(low, 2, chips - 2),
        "beyond": jnp.where(low, chips - 2, 2),
    }[name]
    return lax.rem(chip + step, chips)


def fill_mask(names, chips, local_blocks, chip_ref, core_ref, candidate_ref, mask_ref):
    count = candidate_ref.shape[1]
    own, other = candidate_ref[core_ref[0]], candidate_ref[1 - core_ref[0]]
    held = 0
    for name in names:
        owner = reached(name, chip_ref[0], chips) * CORES + core_ref[0]
        for n in range(local_blocks):
            block = owner * local_blocks + n
            for at, ids in ((0, own), (count, other)):
                here = jnp.where(ids == block, 0.0, FAR).astype(jnp.float32)
                here = jnp.max(here, 1, keepdims=True)
                mask_ref[held, at : at + count, :] = jnp.broadcast_to(here, (count, LANES))
            held += 1


def folded(op, tile):
    parts = [tile[r : r + 8] for r in range(0, tile.shape[0], 8)]
    while len(parts) > 1:
        parts = [op(a, b) for a, b in zip(parts[::2], parts[1::2])]
    return parts[0]


def score_kernel(names, chips, local_blocks, later, *refs):
    chip_ref, core_ref, candidate_ref = refs[:3]
    own_ref, other_ref = refs[3:5]
    shards = list(refs[5 : 5 + len(names)])
    rest = refs[5 + len(names) :]
    copies = []
    if later:
        early_max, early_sum, length_ref, power_ref, max_ref, message_ref = rest[:6]
        sum_ref = rest[6]
    else:
        power_ref, max_ref, sum_ref, kept_ref, centre_ref, semaphores = rest[:6]
        copies = [
            pltpu.make_async_copy(shards[-1], centre_ref, semaphores.at[0]),
            pltpu.make_async_copy(own_ref, kept_ref, semaphores.at[1]),
        ]
        own_ref, shards[-1] = kept_ref, centre_ref
    rows_ref, square_ref, mask_ref, product_ref = rest[-4:]
    half = own_ref.shape[0]
    steps = half // CHUNK
    centre_rows = shards[0].shape[0] // local_blocks
    blocks = len(names) * local_blocks

    for copy in copies:
        copy.start()
    if copies:
        fill_rows(shards[:-1], rows_ref, square_ref, 0)
        copies[0].wait()
        fill_rows(shards[-1:], rows_ref, square_ref, len(shards) - 1)
    else:
        fill_rows(shards, rows_ref, square_ref, 0)

    def multiply(step):
        source, first = (other_ref, step) if step < steps else (own_ref, step - steps)
        if step == steps and copies:
            copies[1].wait()
        product_ref[step % 2] = lax.dot_general(
            rows_ref[...],
            source[first * CHUNK : (first + 1) * CHUNK, :],
            (((1,), (1,)), ((), ())),
            preferred_element_type=jnp.float32,
        )

    multiply(0)
    fill_mask(names, chips, local_blocks, chip_ref, core_ref, candidate_ref, mask_ref)
    for step in range(2 * steps):
        if step + 1 < 2 * steps:
            multiply(step + 1)
        held = product_ref.at[step % 2]
        for n in range(GROUPS):
            lanes = slice(n * LANES, (n + 1) * LANES)
            place = (step * CHUNK + half) % (2 * half) + n * LANES
            q = place // BLOCK
            tops = []
            for b in range(blocks):
                rows = slice(b * centre_rows, (b + 1) * centre_rows)
                bias = square_ref[rows, :] + mask_ref[b, q : q + 1, :]
                logits = held[rows, lanes] * (2.0 * SHARP) + bias
                held[rows, lanes] = logits
                tops.append(folded(jnp.maximum, logits))
            top = tops[0]
            for more in tops[1:]:
                top = jnp.maximum(top, more)
            top = jnp.max(top, 0, keepdims=True)
            total = jnp.zeros((8, LANES), jnp.float32)
            for b in range(blocks):
                rows = slice(b * centre_rows, (b + 1) * centre_rows)
                power = jnp.exp2(held[rows, lanes] - top)
                total += folded(jnp.add, power)
                power_ref[rows, place : place + LANES] = power.astype(jnp.bfloat16)
            group = place // LANES
            max_ref[group : group + 1, :] = top
            sum_ref[group : group + 1, :] = jnp.sum(total, 0, keepdims=True)

    if later:
        both = jnp.maximum(max_ref[...], early_max[...])
        summed = sum_ref[...] * jnp.exp2(max_ref[...] - both)
        summed += early_sum[...] * jnp.exp2(early_max[...] - both)
        lse = both + jnp.log2(summed)
        groups = half // LANES
        here, there = lse[:groups], lse[groups:]
        first = core_ref[0] == 0
        lengths = [
            jnp.full((1, LANES), length_ref[q].astype(jnp.float32)) for q in range(half // BLOCK)
        ]
        lengths += [jnp.zeros((1, LANES), jnp.float32)] * (-len(lengths) % 8)
        message = jnp.concatenate(
            [jnp.where(first, here, there), jnp.where(first, there, here), *lengths], 0
        )
        for n in range(message_ref.shape[0]):
            message_ref[n] = message


def score(names, chips, chip, core, candidates, points, shards, local_blocks, later=None):
    size = shards[0].shape[0]
    half = points[0].shape[0]
    rows = size * len(shards)
    groups = 2 * half // LANES
    stat = jax.ShapeDtypeStruct((groups, LANES), jnp.float32)
    out_shape = [jax.ShapeDtypeStruct((rows, 2 * half), jnp.bfloat16), stat]
    scratch = []
    in_specs = [SMEM, SMEM] + [VMEM] * (3 + len(shards))
    args = [chip, core, candidates, *points, *shards]
    if later is None:
        in_specs[3] = in_specs[-1] = pl.BlockSpec(memory_space=pltpu.HBM)
        out_shape += [stat, jax.ShapeDtypeStruct(points[0].shape, points[0].dtype)]
        scratch += [pltpu.VMEM((size, D), shards[0].dtype), pltpu.SemaphoreType.DMA((2,))]
    else:
        early, lengths, copies = later
        in_specs += [VMEM, VMEM, SMEM]
        args += [*early, lengths]
        spare = -(-(half // BLOCK) // 8) * 8
        out_shape += [jax.ShapeDtypeStruct((copies, groups + spare, LANES), jnp.float32)]
        scratch += [pltpu.VMEM((groups, LANES), jnp.float32)]
    point_blocks = -(-(2 * half // BLOCK) // 8) * 8

    def kernel(*refs):
        score_kernel(names, chips, local_blocks, later is not None, *refs)

    return pl.pallas_call(
        kernel,
        in_specs=in_specs,
        out_specs=[VMEM] * len(out_shape),
        out_shape=out_shape,
        scratch_shapes=scratch
        + [
            pltpu.VMEM((rows, D), jnp.bfloat16),
            pltpu.VMEM((rows, LANES), jnp.float32),
            pltpu.VMEM((len(shards) * local_blocks, point_blocks, LANES), jnp.float32),
            pltpu.VMEM((2, rows, CHUNK), jnp.float32),
        ],
        compiler_params=compiler_params(),
        cost_estimate=pl.CostEstimate(
            flops=2 * rows * 2 * half * D,
            bytes_accessed=2 * half * D * 2 + rows * half * 4,
            transcendentals=rows * 2 * half,
        ),
    )(*args)


def write_message(out, total_ref, mass):
    size = total_ref.shape[0]
    for j in range(D // LANES):
        out[j * size : (j + 1) * size, :] = total_ref[:, j * LANES : (j + 1) * LANES].astype(
            jnp.bfloat16
        )
    coarse = mass.astype(jnp.bfloat16).astype(jnp.float32)
    out[D // LANES * size :, :] = jnp.concatenate([coarse, mass - coarse], 0).astype(jnp.bfloat16)


def merge_kernel(total_ref, mass_ref, arrived_ref, out_ref):
    size = total_ref.shape[0]
    tail = D // LANES * size
    for j in range(D // LANES):
        rows = slice(j * size, (j + 1) * size)
        total = total_ref[:, j * LANES : (j + 1) * LANES] + arrived_ref[rows, :].astype(jnp.float32)
        out_ref[rows, :] = total.astype(jnp.bfloat16)
    sent = arrived_ref[tail:, :].astype(jnp.float32)
    mass = mass_ref[...] + sent[:8] + sent[8:]
    coarse = mass.astype(jnp.bfloat16).astype(jnp.float32)
    out_ref[tail:, :] = jnp.concatenate([coarse, mass - coarse], 0).astype(jnp.bfloat16)


def merged(total, mass, arrived):
    return pl.pallas_call(
        merge_kernel,
        in_specs=[VMEM] * 3,
        out_specs=VMEM,
        out_shape=jax.ShapeDtypeStruct(arrived.shape, arrived.dtype),
        compiler_params=compiler_params(),
    )(total, mass, arrived)


def moments_kernel(sources, sent, size, keep, first, *refs):
    core_ref, all_ref, own_ref, other_ref = refs[:4]
    tops, powers = refs[4:6], refs[6:8]
    outs = refs[8:-4]
    scale_ref, total_ref, mass_ref, weight_ref = refs[-4:]
    half = own_ref.shape[0]
    steps = half // CHUNK
    groups = half // LANES
    at_zero = core_ref[0] == 0

    parts = all_ref[:, : 2 * groups, :]
    top = jnp.max(parts, 0)
    lse = top + jnp.log2(jnp.sum(jnp.exp2(parts - top[None]), 0))
    here = jnp.where(at_zero, lse[:groups], lse[groups:])
    there = jnp.where(at_zero, lse[groups:], lse[:groups])
    for n, top_ref in enumerate(tops):
        scale_ref[n] = jnp.exp2(top_ref[...] - jnp.concatenate([here, there], 0))
    if first:
        outs[-1][...] = here * math.log(2.0)
    copies = all_ref.shape[0] // CORES
    lane = lax.broadcasted_iota(jnp.int32, (1, LANES), 1).astype(jnp.float32)

    def weigh(step):
        for at in range(GROUPS):
            group = step * GROUPS + at
            q = group * LANES // BLOCK
            part = (group * LANES % BLOCK) // LANES
            row = 2 * groups + q % (half // BLOCK)
            zero, one = all_ref[0, row : row + 1, :], all_ref[copies, row : row + 1, :]
            mine = q < half // BLOCK
            length = jnp.where(at_zero, zero if mine else one, one if mine else zero)
            live = jnp.where(lane + part * LANES < length, 1.0, 0.0)
            lanes = slice(group * LANES, (group + 1) * LANES)
            for n, (which, start) in enumerate(sources):
                scale = scale_ref[which, group : group + 1, :] * live
                for r in range(0, size, 64):
                    power = powers[which][start + r : start + r + 64, lanes].astype(jnp.float32)
                    weights = (power * scale).astype(jnp.bfloat16)
                    rows = slice(n * size + r, n * size + r + 64)
                    weight_ref[rows, lanes] = weights
                    if group == 0:
                        mass_ref[rows, :] = weights.astype(jnp.float32)
                    else:
                        mass_ref[rows, :] += weights.astype(jnp.float32)

    weigh(0)
    for step in range(2 * steps):
        if step + 1 < 2 * steps:
            weigh(step + 1)
        source, at = (own_ref, step) if step < steps else (other_ref, step - steps)
        part = jnp.dot(
            weight_ref[:, step * CHUNK : (step + 1) * CHUNK],
            source[at * CHUNK : (at + 1) * CHUNK, :],
            preferred_element_type=jnp.float32,
        )
        if step == 0:
            total_ref[...] = part
        else:
            total_ref[...] += part

    for out, n in zip(outs, sent if keep is None else (*sent, keep)):
        rows = slice(n * size, (n + 1) * size)
        mass = jnp.sum(jnp.transpose(mass_ref[rows, :]), 0, keepdims=True)
        mass = jnp.broadcast_to(mass, (8, size))
        if n == keep:
            out[...] = total_ref[rows, :]
            outs[len(sent) + 1][...] = mass
        else:
            write_message(out, total_ref.at[rows, :], mass)


def moments(core, everyone, points, tops, powers, sources, size, sent, keep, first):
    half = points[0].shape[0]
    rows = len(sources) * size
    groups = 2 * half // LANES
    message = (D // LANES * size + 16, LANES)
    out_shape = [jax.ShapeDtypeStruct(message, jnp.bfloat16)] * len(sent)
    if keep is not None:
        out_shape += [
            jax.ShapeDtypeStruct((size, D), jnp.float32),
            jax.ShapeDtypeStruct((8, size), jnp.float32),
        ]
    if first:
        out_shape += [jax.ShapeDtypeStruct((half // LANES, LANES), jnp.float32)]

    def kernel(*refs):
        moments_kernel(sources, sent, size, keep, first, *refs)

    return pl.pallas_call(
        kernel,
        in_specs=[SMEM] + [VMEM] * 7,
        out_specs=[VMEM] * len(out_shape),
        out_shape=out_shape,
        scratch_shapes=[
            pltpu.VMEM((len(tops), groups, LANES), jnp.float32),
            pltpu.VMEM((rows, D), jnp.float32),
            pltpu.VMEM((rows, LANES), jnp.float32),
            pltpu.VMEM((rows, 2 * half), jnp.bfloat16),
        ],
        compiler_params=compiler_params(),
        cost_estimate=pl.CostEstimate(
            flops=2 * rows * 2 * half * D,
            bytes_accessed=2 * half * D * 2 + rows * half * 4,
            transcendentals=0,
        ),
    )(core, everyone, *points, *tops, *powers)


def finish_kernel(*refs):
    home_ref, home_mass_ref, centre_ref = refs[:3]
    arrived = refs[3:-2]
    updated_ref, mass_out_ref = refs[-2:]
    size = centre_ref.shape[0]
    tail = D // LANES * size
    mass = home_mass_ref[...]
    for message in arrived:
        sent = message[tail:, :].astype(jnp.float32)
        mass += sent[:8] + sent[8:]
    rows, width = mass_out_ref.shape
    for n in range(rows):
        mass_out_ref[n : n + 1, :] = mass[:1, n * width : (n + 1) * width]
    inverse = 1.0 / (mass[:1] + prior_mass)
    inverse = jnp.transpose(jnp.broadcast_to(inverse, (LANES, size)))
    for j in range(D // LANES):
        lanes = slice(j * LANES, (j + 1) * LANES)
        total = home_ref[:, lanes] + prior_mass * centre_ref[:, lanes].astype(jnp.float32)
        for message in arrived:
            total += message[j * size : (j + 1) * size, :].astype(jnp.float32)
        updated_ref[:, lanes] = (total * inverse).astype(jnp.bfloat16)


def finish(home, home_mass, centre, arrived, local_blocks):
    size = centre.shape[0]
    return pl.pallas_call(
        finish_kernel,
        in_specs=[VMEM] * (3 + len(arrived)),
        out_specs=[VMEM] * 2,
        out_shape=[
            jax.ShapeDtypeStruct((size, D), jnp.bfloat16),
            jax.ShapeDtypeStruct((local_blocks, size // local_blocks), jnp.float32),
        ],
        compiler_params=compiler_params(),
    )(home, home_mass, centre, *arrived)


def local(points, lengths, candidates, centroids):
    chips = lax.axis_size("chip")
    copies = CORES * lax.axis_size("cen")
    chip = lax.axis_index("chip").astype(jnp.int32).reshape(1)
    core = lax.axis_index("core").astype(jnp.int32).reshape(1)
    local_blocks, centre_rows, _ = centroids.shape
    size = local_blocks * centre_rows

    def moved(value, step):
        return lax.ppermute(value, "chip", [(c, step(c) % chips) for c in range(chips)])

    def ahead(c):
        return c + 1

    def back(c):
        return c - 1

    def across(c):
        return c // ROW * ROW + (c + ROW // 2) % ROW

    def outward(c):
        return c + ROW if c % ROW < ROW // 2 else c - ROW

    def inward(c):
        return c - ROW if c % ROW < ROW // 2 else c + ROW

    def swapped(value):
        return lax.ppermute(value, "core", [(0, 1), (1, 0)])

    centre = centroids.reshape(size, D)
    row = moved(centre, across)
    near = [moved(centre, ahead), moved(centre, back)]
    beyond = moved(row, outward)
    other = swapped(points)
    candidates = lax.all_gather(candidates, "core")

    first_power, first_max, first_sum, kept = score(
        ("row", "own"),
        chips,
        chip,
        core,
        candidates,
        [pltpu.with_memory_space_constraint(points, pltpu.HBM), other],
        [row, pltpu.with_memory_space_constraint(centre, pltpu.HBM)],
        local_blocks,
    )
    points = [kept, other]
    last_power, last_max, message = score(
        ("before", "after", "beyond"),
        chips,
        chip,
        core,
        candidates,
        points,
        [*near, beyond],
        local_blocks,
        ((first_max, first_sum), lengths, copies),
    )
    everyone = lax.all_to_all(message, ("core", "cen"), 0, 0)
    tops, powers = (first_max, last_max), (first_power, last_power)
    beyond, lse = moments(
        core, everyone, points, tops, powers, ((1, 2 * size),), size, (0,), None, True
    )
    beyond = moved(beyond, inward)
    before, after, row, row_mass = moments(
        core, everyone, points, tops, powers, ((1, 0), (1, size), (0, 0)), size, (0, 1), 2, False
    )
    arrived = [moved(after, ahead), moved(before, back)]
    arrived += [moved(merged(row, row_mass, beyond), across)]
    home, home_mass = moments(
        core, everyone, points, tops, powers, ((0, size),), size, (), 0, False
    )
    updated, masses = finish(home, home_mass, centre, arrived, local_blocks)
    return updated.reshape(centroids.shape), masses, lse.reshape(-1)


def solution(mesh):
    pt, cen = mesh.axis_names
    split = Mesh(
        mesh.devices.reshape(mesh.shape[pt] // CORES, CORES, mesh.shape[cen]),
        ("chip", "core", "cen"),
    )
    whole_pt = ("chip", "core")
    return jax.shard_map(
        local,
        mesh=split,
        in_specs=(P(whole_pt, None), P(whole_pt), P(whole_pt, None), P(whole_pt, "cen", None)),
        out_specs=(P(whole_pt, "cen", None), P(whole_pt, "cen"), P(whole_pt)),
        check_vma=False,
    )
```
